32 devices in a mesh: dp: 16 (over z, y, x), tensor: 2 (over core).
Axes of the slice: x: 2, y: 2, z: 4, core: 2. Of those that a mesh axis runs over, the one named last changes fastest.
Arguments:
- tokens: bfloat16 [32768, 768], P('dp')
- cotangent: bfloat16 [32768, 768], P('dp'), may hold values from -6 to 6
- pair_lengths: int32 [32, 8], P('dp'), may hold values from 1 to 1017, as said below
- mat_master: float32 [768, 96, 96], P(('dp', 'tensor'))
- mat_left: float32 [768, 96, 96], P(('dp', 'tensor')), as said below
- mat_right: float32 [768, 96, 96], P(('dp', 'tensor')), as said below
- root_left: float32 [768, 96, 96], P(('dp', 'tensor'))
- root_right: float32 [768, 96, 96], P(('dp', 'tensor'))
- vec_master: float32 [9216], P(('dp', 'tensor'))
- vec_second: float32 [9216], P(('dp', 'tensor'))
Outputs:
- block_out: bfloat16 [32768, 768], P('dp')
- input_grad: float32 [32768, 768], P('dp')
- mat_grads: float32 [768, 96, 96], P(('dp', 'tensor'))
- mat_left_new: float32 [768, 96, 96], P(('dp', 'tensor'))
- mat_right_new: float32 [768, 96, 96], P(('dp', 'tensor'))
- mat_new: float32 [768, 96, 96], P(('dp', 'tensor'))
- vec_grads: float32 [9216], P(('dp', 'tensor'))
- vec_second_new: float32 [9216], P(('dp', 'tensor'))
- vec_new: float32 [9216], P(('dp', 'tensor'))
- stream_rms: float32 [3], replicated
The draws below stay inside these ranges and needn't reach their ends.
Inputs may be any that keep to these rules, and one draw needn't show every extreme that they name: `pair_lengths`: in each row the 8 lengths add up to at most 1024; the positions after them are padding. `mat_left`: each block is symmetric. `mat_right`: each block is symmetric.
All inputs are finite; a program needn't handle non-finite values.
Results may differ from the reference program's by a relative error of at most 0.017.
Values may be sent and summed in bfloat16 or wider, within the bound.
A program may use at most 192 MiB of HBM per device.

```python
import math
from functools import partial
import jax
import jax.numpy as jnp
from jax import lax

D = 768
H = 12
HD = 64
FF = 3072
SEQ = 1024
PAIRS = 8
BS = 96
ROWS = 32
TOKENS = 32768
KB = 128
BPD = 8
NBLK = 768
VEC = 9216
VS = 288
N_DP = 16


GRAD_SHARE = (0.1, 0.1, 0.3, 0.01, 0.15, 0.15)


VEC_SHARE = (0.1, 0.3, 0.15, 0.15, 0.15, 0.15, 0.5, 0.5, 0.7, 0.7, 0.7, 0.7)


OFF_SHARE = 0.1


def weight_scales():
    inner = D ** (-0.5)
    return jnp.array([inner, inner, inner, 6.0 * inner, inner, FF ** (-0.5)], dtype=jnp.float32)


def block_kinds():
    index = jnp.arange(NBLK, dtype=jnp.int32)
    kind = index // BPD % 3
    within = index // (6 * BPD) * BPD + index % BPD
    return jnp.where(kind == 0, within // (KB // 4), kind + 3)


def vector_pieces():
    index = jnp.arange(VEC, dtype=jnp.int32)
    place = index // (2 * VS) * VS + index % VS
    return place // (D // 2)


def log_spread(key, shape, lower, upper):
    return jnp.exp(jax.random.uniform(key, shape, minval=math.log(lower), maxval=math.log(upper)))


def definite(key, scales, lower, upper):
    diagonal_key, noise_key = jax.random.split(key)
    diagonal = log_spread(diagonal_key, (NBLK, BS), lower, upper)
    noise = jax.random.normal(noise_key, (NBLK, BS, BS))
    noise = 0.5 * (noise + jnp.swapaxes(noise, 1, 2))
    identity = jnp.eye(BS, dtype=jnp.float32)
    return scales[:, None, None] * (identity[None] * diagonal[:, :, None] + OFF_SHARE * (1.0 - identity)[None] * noise)


def stat_scales():
    return BS * TOKENS * jnp.array(GRAD_SHARE, dtype=jnp.float32)[block_kinds()]


def root_scales():
    kinds = block_kinds()
    share = jnp.array(GRAD_SHARE, dtype=jnp.float32)[kinds]
    return jnp.sqrt(weight_scales()[kinds]) * (share * TOKENS) ** (-0.25)


def draw_tokens(key, part):
    base_key = jax.random.fold_in(key, 8)
    return jnp.clip(jax.random.normal(base_key, (TOKENS, D)), -6.0, 6.0).astype(jnp.bfloat16)


def draw_pair_lengths(key, part):
    base_key = jax.random.fold_in(key, 9)
    noise_key, weight_key, place_key = jax.random.split(base_key, 3)
    rows = jnp.arange(ROWS, dtype=jnp.int32)
    third = SEQ // 3
    target = third + (SEQ - third) * rows // max(ROWS - 1, 1)
    noise = jax.random.randint(noise_key, (ROWS,), -(SEQ // 16), SEQ // 16 + 1)
    target = jnp.clip(target + noise, PAIRS, SEQ)
    target = jnp.where(rows == ROWS - 1, SEQ, target)
    weights = jax.random.randint(weight_key, (ROWS, PAIRS), 1, 32)
    ends = jnp.cumsum(weights, axis=1)
    spare = (target - PAIRS)[:, None]
    bounds = spare * ends // ends[:, -1:]
    before = jnp.concatenate([jnp.zeros((ROWS, 1), jnp.int32), bounds[:, :-1]], axis=1)
    lengths = (1 + bounds - before).astype(jnp.int32)
    place = jax.random.randint(place_key, (), 0, PAIRS)
    columns = jnp.arange(PAIRS, dtype=jnp.int32)
    last_row = jnp.where(columns == place, SEQ - PAIRS + 1, 1).astype(jnp.int32)
    return jnp.where((rows == ROWS - 1)[:, None], last_row[None, :], lengths).astype(jnp.int32)


def draw_mat_master(key, part):
    base_key = jax.random.fold_in(key, 5)
    scales = weight_scales()[block_kinds()][:, None, None]
    base = jnp.clip(jax.random.normal(base_key, (NBLK, BS, BS)), -4.0, 4.0)
    return (scales * base).astype(jnp.float32)


def draw_mat_left(key, part):
    return definite(jax.random.fold_in(key, 1), stat_scales(), 1.0, 4.0)


def draw_mat_right(key, part):
    return definite(jax.random.fold_in(key, 2), stat_scales(), 1.0, 4.0)


def draw_root_left(key, part):
    return definite(jax.random.fold_in(key, 3), root_scales(), 0.5, 2.0)


def draw_root_right(key, part):
    return definite(jax.random.fold_in(key, 4), root_scales(), 0.5, 2.0)


def draw_vec_master(key, part):
    gain_key, bias_key = jax.random.split(jax.random.fold_in(key, 6))
    pieces = vector_pieces()
    gains = jax.random.uniform(gain_key, (VEC,), minval=0.6, maxval=1.4)
    biases = 0.2 * jnp.clip(jax.random.normal(bias_key, (VEC,)), -4.0, 4.0)
    return jnp.where((pieces == 8) | (pieces == 10), gains, biases).astype(jnp.float32)


def draw_vec_second(key, part):
    share = jnp.array(VEC_SHARE, dtype=jnp.float32)[vector_pieces()]
    return (share * TOKENS * log_spread(jax.random.fold_in(key, 7), (VEC,), 1.0, 4.0)).astype(jnp.float32)


def level_of(rng, dims, cuts, low, largest):
    factor_of = 1.0
    for axis_at, blocks in cuts:
        draws = jax.random.uniform(jax.random.fold_in(jax.random.fold_in(rng, 6), axis_at), (blocks,), jnp.float32, low / len(cuts), largest / len(cuts))
        factor_of = factor_of * jnp.repeat(jnp.exp(draws), dims[axis_at] // blocks).reshape((-1,) + (1,) * (len(dims) - 1 - axis_at))
    return factor_of


def bell_draw(key, shape, scale, bound, cuts=(), held_as=jnp.bfloat16):
    factor_of = level_of(key, shape, cuts, -0.22, 0.18) if cuts else 1.0
    entries = jax.random.normal(key, shape, jnp.float32) * scale * factor_of
    return jnp.minimum(jnp.maximum(entries, -bound), bound).astype(held_as)


def setup_inputs(seed: int = 0) -> dict:
    key_list = jax.random.split(jax.random.key(seed), 11)
    return {
        "tokens": draw_tokens(jax.random.fold_in(key_list[10], 71), 0),
        "cotangent": bell_draw(key_list[1], (TOKENS, D), 1.0, 6.0, ((0, 16),)),
        "pair_lengths": draw_pair_lengths(jax.random.fold_in(key_list[10], 71), 0),
        "mat_master": draw_mat_master(jax.random.fold_in(key_list[10], 71), 0),
        "mat_left": draw_mat_left(jax.random.fold_in(key_list[10], 71), 0),
        "mat_right": draw_mat_right(jax.random.fold_in(key_list[10], 71), 0),
        "root_left": draw_root_left(jax.random.fold_in(key_list[10], 71), 0),
        "root_right": draw_root_right(jax.random.fold_in(key_list[10], 71), 0),
        "vec_master": draw_vec_master(jax.random.fold_in(key_list[10], 71), 0),
        "vec_second": draw_vec_second(jax.random.fold_in(key_list[10], 71), 0),
    }


LN_EPS = 1e-12
NEG_FILL = -1e+30
DECAY = 0.5
STEP_RATE = 1.0
VEC_RATE = 0.1
VEC_EPS = 1e-08
HIGHEST = lax.Precision.HIGHEST

@jax.custom_vjp
def low(v):
    return lax.optimization_barrier(v.astype(jnp.bfloat16)).astype(jnp.float32)

@jax.custom_vjp
def low_back(v):
    return v

def low_keep(v):
    return (low(v), None)

def low_pass(kept, grad):
    return (grad,)

def back_keep(v):
    return (v, None)

def back_low(kept, grad):
    return (low(grad),)
low.defvjp(low_keep, low_pass)
low_back.defvjp(back_keep, back_low)

def product(left, right):
    return jnp.dot(left, right, precision=HIGHEST, preferred_element_type=jnp.float32)

def unblock(blocks, grid_rows, grid_cols):
    edge = blocks.shape[-1]
    return blocks.reshape(grid_rows, grid_cols, edge, edge).transpose(0, 2, 1, 3).reshape(grid_rows * edge, grid_cols * edge)

def to_blocks(matrix, edge):
    grid_rows = matrix.shape[0] // edge
    grid_cols = matrix.shape[1] // edge
    return matrix.reshape(grid_rows, edge, grid_cols, edge).transpose(0, 2, 1, 3).reshape(grid_rows * grid_cols, edge, edge)

def half_kinds(matrices, part):
    return matrices.reshape(N_DP, 2, 3, BPD, BS, BS)[:, part].transpose(1, 0, 2, 3, 4).reshape(3, KB, BS, BS)

def full_weights(matrices):
    grid_model = D // BS
    grid_half = D // (2 * BS)
    grid_hidden = FF // (2 * BS)
    quarter = KB // 4
    halves = [half_kinds(matrices, part) for part in range(2)]
    pieces = []
    for number in range(3):
        pieces.append(jnp.concatenate([unblock(kinds[0, number * quarter:(number + 1) * quarter], grid_model, grid_half) for kinds in halves], axis=1))
    pieces.append(jnp.concatenate([unblock(kinds[0, 3 * quarter:], grid_half, grid_model) for kinds in halves], axis=0))
    pieces.append(jnp.concatenate([unblock(kinds[1], grid_model, grid_hidden) for kinds in halves], axis=1))
    pieces.append(jnp.concatenate([unblock(kinds[2], grid_hidden, grid_model) for kinds in halves], axis=0))
    return pieces

def pack_weights(matrices):
    half = D // 2
    hidden_half = FF // 2
    parts = []
    for part in range(2):
        span = slice(part * half, (part + 1) * half)
        hidden_span = slice(part * hidden_half, (part + 1) * hidden_half)
        attention_blocks = jnp.concatenate([to_blocks(matrices[0][:, span], BS), to_blocks(matrices[1][:, span], BS), to_blocks(matrices[2][:, span], BS), to_blocks(matrices[3][span], BS)], axis=0)
        up_blocks = to_blocks(matrices[4][:, hidden_span], BS)
        down_blocks = to_blocks(matrices[5][hidden_span], BS)
        kinds = jnp.stack([attention_blocks, up_blocks, down_blocks]).reshape(3, N_DP, BPD, BS, BS).transpose(1, 0, 2, 3, 4)
        parts.append(kinds)
    return jnp.stack(parts, axis=1).reshape(NBLK, BS, BS)

def full_vectors(vector):
    halves = vector.reshape(N_DP, 2, VS).transpose(1, 0, 2).reshape(2, 12, D // 2)
    bias_query = jnp.concatenate([halves[0, 0], halves[1, 0]])
    bias_value = jnp.concatenate([halves[0, 1], halves[1, 1]])
    bias_up = jnp.concatenate([halves[0, 2:6].reshape(-1), halves[1, 2:6].reshape(-1)])
    shared = jnp.concatenate([halves[0, 6:], halves[1, 6:]], axis=1)
    return [bias_query, bias_value, bias_up, shared[0], shared[1], shared[2], shared[3], shared[4], shared[5]]

def pack_vectors(vectors):
    half = D // 2
    hidden_half = FF // 2
    parts = []
    for part in range(2):
        span = slice(part * half, (part + 1) * half)
        pieces = [vectors[0][span], vectors[1][span], vectors[2][part * hidden_half:(part + 1) * hidden_half]]
        pieces = pieces + [entry[span] for entry in vectors[3:]]
        parts.append(jnp.concatenate(pieces).reshape(N_DP, VS))
    return jnp.stack(parts, axis=1).reshape(VEC)

def pair_index(lengths, seq_len):
    ends = jnp.cumsum(lengths, axis=-1)
    places = lax.broadcasted_iota(jnp.int32, (lengths.shape[0], seq_len, 1), 1)
    return lax.optimization_barrier(jnp.sum((places >= ends[:, None, :]).astype(jnp.int32), axis=-1))

def layer_norm(residual, gain, shift):
    centred = residual - lax.optimization_barrier(jnp.mean(residual, axis=-1, keepdims=True))
    inverse_spread = lax.rsqrt(lax.optimization_barrier(jnp.mean(centred * centred, axis=-1, keepdims=True)) + LN_EPS)
    return centred * inverse_spread * gain + shift

def row_attention(items):
    queries, keys, values, pair_row = items
    scores = jnp.einsum('qhd,khd->hqk', queries, keys, precision=HIGHEST) * HD ** (-0.5)
    scores = low_back(scores)
    allowed = ((pair_row[:, None] == pair_row[None, :]) & (pair_row[None, :] < PAIRS))[None]
    masked = jnp.where(allowed, scores, NEG_FILL)
    top = lax.optimization_barrier(jnp.max(masked, axis=-1, keepdims=True))
    weights = jnp.where(allowed, jnp.exp(masked - top), 0.0)
    total = jnp.maximum(lax.optimization_barrier(jnp.sum(weights, axis=-1, keepdims=True)), 0.5)
    probs = low(weights / total)
    context = jnp.einsum('hqk,khd->qhd', probs, values, precision=HIGHEST)
    return low_back(low(context))

def forward(x_float, w_query, w_key, w_value, w_out, w_up, w_down, bias_query, bias_value, bias_up, bias_out, bias_down, gain_one, shift_one, gain_two, shift_two, pairs, valid):
    half = D // 2
    hidden_half = FF // 2
    w_query, w_key, w_value, w_out, w_up, w_down = [low(weight) for weight in (w_query, w_key, w_value, w_out, w_up, w_down)]
    queries = low(low_back(product(x_float, w_query)) + bias_query)
    keys = low(low_back(product(x_float, w_key)))
    values = low(low_back(product(x_float, w_value)) + bias_value)
    shape_four = (ROWS, SEQ, H, HD)
    context = lax.map(jax.checkpoint(row_attention), (queries.reshape(shape_four), keys.reshape(shape_four), values.reshape(shape_four), pairs))
    context = context.reshape(TOKENS, D)
    first = low(product(context[:, :half], w_out[:half]))
    second = low(product(context[:, half:], w_out[half:]))
    attention = low_back(first + second) + bias_out
    residual_one = x_float + attention
    hidden = layer_norm(residual_one, gain_one, shift_one)
    hidden_low = low(hidden)
    pre_act = low_back(product(hidden_low, w_up)) + bias_up
    act_low = low(jax.nn.gelu(pre_act, approximate=False))
    first_feed = low(product(act_low[:, :hidden_half], w_down[:hidden_half]))
    second_feed = low(product(act_low[:, hidden_half:], w_down[hidden_half:]))
    feed = low_back(first_feed + second_feed) + bias_down
    residual_two = hidden + feed
    output = layer_norm(residual_two, gain_two, shift_two)
    mask = valid[:, None]
    sums = jnp.stack([jnp.sum(mask * residual_one * residual_one), jnp.sum(mask * attention * attention), jnp.sum(mask * feed * feed)])
    return (output, sums)

def reference(tokens, cotangent, pair_lengths, mat_master, mat_left, mat_right, root_left, root_right, vec_master, vec_second):
    pairs = pair_index(pair_lengths, SEQ)
    valid = (pairs < PAIRS).astype(jnp.float32).reshape(TOKENS)
    weights = full_weights(mat_master)
    vectors = full_vectors(vec_master)
    x_float = tokens.astype(jnp.float32)
    closed = partial(forward, pairs=pairs, valid=valid)
    output, pullback, sums = jax.vjp(closed, x_float, *weights, *vectors, has_aux=True)
    grad_out = cotangent.astype(jnp.float32) * valid[:, None]
    grads = pullback(grad_out)
    input_grad = grads[0]
    mat_grads = pack_weights(grads[1:7])
    vec_grads = pack_vectors(grads[7:16])
    count = jnp.sum(valid)
    stream_rms = jnp.sqrt(sums / (count * D))
    left_new = DECAY * mat_left + (1.0 - DECAY) * jnp.einsum('bij,bkj->bik', mat_grads, mat_grads, precision=HIGHEST)
    right_new = DECAY * mat_right + (1.0 - DECAY) * jnp.einsum('bji,bjk->bik', mat_grads, mat_grads, precision=HIGHEST)
    turned = jnp.einsum('bij,bjk->bik', root_left, mat_grads, precision=HIGHEST)
    turned = jnp.einsum('bij,bjk->bik', turned, root_right, precision=HIGHEST)
    mat_new = mat_master - STEP_RATE * turned
    second_new = DECAY * vec_second + (1.0 - DECAY) * vec_grads * vec_grads
    vec_new = vec_master - VEC_RATE * vec_grads / (jnp.sqrt(second_new) + VEC_EPS)
    return (output.astype(jnp.bfloat16), input_grad, mat_grads, left_new, right_new, mat_new, vec_grads, second_new, vec_new, stream_rms)
```

```python
from functools import partial
import math

import jax
import jax.numpy as jnp
from jax import lax
from jax.experimental import pallas as pl
from jax.experimental.pallas import tpu as pltpu
from jax.sharding import PartitionSpec as P

HD = 64
LN_EPS = 1e-12
BIG = 1e30
FLOOR = -1e29
DECAY = 0.5
STEP_RATE = 1.0
VEC_RATE = 0.1
VEC_EPS = 1e-08
INV_ROOT_TWO = 1.0 / math.sqrt(2.0)
INV_ROOT_TWO_PI = 1.0 / math.sqrt(2.0 * math.pi)
BF = jnp.bfloat16
F32 = jnp.float32
LANES = 128
VMEM_LIMIT = 60 * 2**20
MESH = pl.DeviceIdType.MESH


def nn(a, b):
    return lax.dot_general(a, b, (((1,), (0,)), ((), ())), preferred_element_type=F32)


def nt(a, b):
    return lax.dot_general(a, b, (((1,), (1,)), ((), ())), preferred_element_type=F32)


def tn(a, b):
    return lax.dot_general(a, b, (((0,), (0,)), ((), ())), preferred_element_type=F32)


def unblock(blocks, grid_rows, grid_cols):
    edge = blocks.shape[-1]
    return (
        blocks.reshape(grid_rows, grid_cols, edge, edge)
        .transpose(0, 2, 1, 3)
        .reshape(grid_rows * edge, grid_cols * edge)
    )


def to_blocks(matrix, edge):
    grid_rows = matrix.shape[0] // edge
    grid_cols = matrix.shape[1] // edge
    return (
        matrix.reshape(grid_rows, edge, grid_cols, edge)
        .transpose(0, 2, 1, 3)
        .reshape(grid_rows * grid_cols, edge, edge)
    )


def erf_parts(u):
    z = jnp.abs(u) * INV_ROOT_TWO
    gauss = jnp.exp(-z * z)
    t = 1.0 / (1.0 + 0.3275911 * z)
    poly = t * (
        0.254829592
        + t * (-0.284496736 + t * (1.421413741 + t * (-1.453152027 + t * 1.061405429)))
    )
    tail = poly * gauss
    return jnp.where(u >= 0.0, 2.0 - tail, tail), gauss


def params(**kw):
    return pltpu.CompilerParams(vmem_limit_bytes=VMEM_LIMIT, **kw)


def low_lanes(shape):
    return lax.broadcasted_iota(jnp.int32, shape, 1) < HD


def attn_fwd_kernel(
    tok, w_qkv, w_out, bias, hot, cold, qkv, ctx, lse, part, *, half, seq, blk
):
    heads = half // HD
    qkv[...] = (nn(tok[...], w_qkv[...]) + bias[...]).astype(BF)
    low = low_lanes((blk, LANES))
    lane = lax.broadcasted_iota(jnp.int32, (blk, LANES), 1)

    def step(index, carry):
        rows = pl.ds(pl.multiple_of(index * blk, blk), blk)
        hot_blk = hot[0, rows, :]
        stats = jnp.zeros((blk, LANES), F32)
        for pair in range(heads // 2):
            cols = pl.ds(pair * LANES, LANES)
            q_pair = qkv[rows, cols] * jnp.asarray(HD**-0.5, BF)
            k_aug = jnp.concatenate(
                [qkv[:, pl.ds(half + pair * LANES, LANES)], cold[0]], axis=1
            )
            v_pair = qkv[:, pl.ds(2 * half + pair * LANES, LANES)]
            outs = []
            for side in range(2):
                own = low if side == 0 else jnp.logical_not(low)
                q_aug = jnp.concatenate([jnp.where(own, q_pair, 0), hot_blk], axis=1)
                s = nt(q_aug, k_aug)
                top = jnp.maximum(jnp.max(s, axis=1, keepdims=True), FLOOR)
                e = jnp.exp(s - top)
                total = jnp.maximum(jnp.sum(e, axis=1, keepdims=True), 0.5)
                outs.append(nn(e.astype(BF), v_pair) / total)
                stats = jnp.where(lane == 2 * pair + side, top + jnp.log(total), stats)
            ctx[rows, cols] = jnp.where(low, outs[0], outs[1]).astype(BF)
        lse[0, :, rows] = stats.T[: lse.shape[1]]
        return carry

    lax.fori_loop(0, seq // blk, step, 0)
    part[...] = nn(ctx[...], w_out[...]).astype(BF)


def attn_fwd(tok, w_qkv, w_out, bias, hot, cold, rows, seq):
    width = tok.shape[1]
    half = width // 2
    stat_rows = -(-(half // HD) // 8) * 8
    whole = lambda shape: pl.BlockSpec(shape, lambda r: (0,) * len(shape))
    return pl.pallas_call(
        partial(attn_fwd_kernel, half=half, seq=seq, blk=256),
        grid=(rows,),
        in_specs=[
            pl.BlockSpec((seq, width), lambda r: (r, 0)),
            whole((width, 3 * half)),
            whole((half, width)),
            whole((1, 3 * half)),
            pl.BlockSpec((1, seq, LANES), lambda r: (r, 0, 0)),
            pl.BlockSpec((1, seq, LANES), lambda r: (r, 0, 0)),
        ],
        out_specs=[
            pl.BlockSpec((seq, 3 * half), lambda r: (r, 0)),
            pl.BlockSpec((seq, half), lambda r: (r, 0)),
            pl.BlockSpec((1, stat_rows, seq), lambda r: (r, 0, 0)),
            pl.BlockSpec((seq, width), lambda r: (r, 0)),
        ],
        out_shape=[
            jax.ShapeDtypeStruct((rows * seq, 3 * half), BF),
            jax.ShapeDtypeStruct((rows * seq, half), BF),
            jax.ShapeDtypeStruct((rows, stat_rows, seq), F32),
            jax.ShapeDtypeStruct((rows * seq, width), BF),
        ],
        compiler_params=params(),
        name="attn_fwd",
    )(tok, w_qkv, w_out, bias, hot, cold)


def attn_bwd_kernel(
    gattn, qkv, ctx, lse, w_qkv, w_out, hot, cold, gqkv, sums, part, gctx, centre, dk, dv,
    *, half, seq, blk,
):
    heads = half // HD
    g = nt(gattn[...], w_out[...])
    gctx[...] = g.astype(BF)
    prod = gctx[...].astype(F32) * ctx[...].astype(F32)
    picks = (
        lax.broadcasted_iota(jnp.int32, (8, half), 0)
        == lax.broadcasted_iota(jnp.int32, (8, half), 1) // HD
    ).astype(F32)
    centre[...] = lax.dot_general(
        picks, prod, (((1,), (1,)), ((), ())),
        preferred_element_type=F32, precision=lax.Precision.HIGHEST,
    )
    low = low_lanes((blk, LANES))
    scale = jnp.asarray(HD**-0.5, BF)
    for pair in range(heads // 2):
        cols = pl.ds(pair * LANES, LANES)
        dk[...] = jnp.zeros_like(dk)
        dv[...] = jnp.zeros_like(dv)

        def step(index, gq_sum):
            rows = pl.ds(pl.multiple_of(index * blk, blk), blk)
            hot_blk = hot[0, rows, :]
            q_pair = qkv[rows, cols] * scale
            g_pair = gctx[rows, cols]
            k_pair = qkv[:, pl.ds(half + pair * LANES, LANES)]
            k_aug = jnp.concatenate([k_pair, cold[0]], axis=1)
            v_pair = qkv[:, pl.ds(2 * half + pair * LANES, LANES)]
            outs = []
            dk_new = dk[...]
            dv_new = dv[...]
            for side in range(2):
                head = 2 * pair + side
                own = low if side == 0 else jnp.logical_not(low)
                q_own = jnp.where(own, q_pair, 0)
                g_own = jnp.where(own, g_pair, 0)
                s = nt(k_aug, jnp.concatenate([q_own, hot_blk], axis=1))
                p = jnp.exp(s - lse[0, pl.ds(head, 1), rows])
                gp = nt(v_pair, g_own)
                gs = (p * (gp - centre[pl.ds(head, 1), rows])).astype(BF)
                dv_new = dv_new + nn(p.astype(BF), g_own)
                dk_new = dk_new + nn(gs, q_own)
                outs.append(tn(gs, k_pair))
            dk[...] = dk_new
            dv[...] = dv_new
            gq = jnp.where(low, outs[0], outs[1]) * HD**-0.5
            gqkv[rows, cols] = gq.astype(BF)
            return gq_sum + jnp.sum(gq, axis=0, keepdims=True)

        gq_sum = lax.fori_loop(0, seq // blk, step, jnp.zeros((1, LANES), F32))
        gqkv[:, pl.ds(half + pair * LANES, LANES)] = dk[...].astype(BF)
        gqkv[:, pl.ds(2 * half + pair * LANES, LANES)] = dv[...].astype(BF)
        sums[0, 0:1, cols] = gq_sum
        sums[0, 1:2, cols] = jnp.sum(dv[...], axis=0, keepdims=True)
    part[...] = nt(gqkv[...], w_qkv[...]).astype(BF)


def attn_bwd(gattn, qkv, ctx, lse, w_qkv, w_out, hot, cold, rows, seq):
    width = gattn.shape[1]
    half = width // 2
    whole = lambda shape: pl.BlockSpec(shape, lambda r: (0,) * len(shape))
    return pl.pallas_call(
        partial(attn_bwd_kernel, half=half, seq=seq, blk=256),
        grid=(rows,),
        in_specs=[
            pl.BlockSpec((seq, width), lambda r: (r, 0)),
            pl.BlockSpec((seq, 3 * half), lambda r: (r, 0)),
            pl.BlockSpec((seq, half), lambda r: (r, 0)),
            pl.BlockSpec((1, lse.shape[1], seq), lambda r: (r, 0, 0)),
            whole((width, 3 * half)),
            whole((half, width)),
            pl.BlockSpec((1, seq, LANES), lambda r: (r, 0, 0)),
            pl.BlockSpec((1, seq, LANES), lambda r: (r, 0, 0)),
        ],
        out_specs=[
            pl.BlockSpec((seq, 3 * half), lambda r: (r, 0)),
            pl.BlockSpec((1, 8, half), lambda r: (r, 0, 0)),
            pl.BlockSpec((seq, width), lambda r: (r, 0)),
        ],
        out_shape=[
            jax.ShapeDtypeStruct((rows * seq, 3 * half), BF),
            jax.ShapeDtypeStruct((rows, 8, half), F32),
            jax.ShapeDtypeStruct((rows * seq, width), BF),
        ],
        scratch_shapes=[
            pltpu.VMEM((seq, half), BF),
            pltpu.VMEM((8, seq), F32),
            pltpu.VMEM((seq, LANES), F32),
            pltpu.VMEM((seq, LANES), F32),
        ],
        compiler_params=params(),
        name="attn_bwd",
    )(gattn, qkv, ctx, lse, w_qkv, w_out, hot, cold)


def mean_last(x):
    return jnp.mean(x, axis=-1, keepdims=True)


def norm_back(grad, normal, inverse, gain):
    scaled = grad * gain
    return inverse * (scaled - mean_last(scaled) - normal * mean_last(scaled * normal))


def fold(x):
    return jnp.sum(x, axis=0, keepdims=True)


def feed_kernel(
    tok, cot, valid, part, part_all, w_up, w_down, b_up, vec,
    out, r1_grad, gattn, act, hid, gfeed, gpre, sums, up_sum,
    got1, send2, got2, send3, got3, normal1, inv1, grad2, slope, send_sem, recv_sem,
    *, tiles, blk,
):
    i = pl.program_id(0)
    other = 1 - lax.axis_index("tensor")
    width = tok.shape[1]
    hidden = w_up.shape[1]
    chunk = width

    def span(t):
        return pl.ds(pl.multiple_of(t * blk, blk), blk)

    def copy(stage, t):
        src = (part_all, send2, send3)[stage]
        dst = (got1, got2, got3)[stage]
        return pltpu.make_async_remote_copy(
            src_ref=src.at[span(t)],
            dst_ref=dst.at[span(t)],
            send_sem=send_sem.at[stage, t],
            recv_sem=recv_sem.at[stage, t],
            device_id={"tensor": other},
            device_id_type=MESH,
        )

    @pl.when(i == 0)
    def _():
        barrier = pltpu.get_barrier_semaphore()
        pl.semaphore_signal(barrier, inc=1, device_id={"tensor": other}, device_id_type=MESH)
        pl.semaphore_wait(barrier, 1)
        for t in range(tiles):
            copy(0, t).start()
        sums[...] = jnp.zeros_like(sums)
        up_sum[...] = jnp.zeros_like(up_sum)

    bias_out, bias_down = vec[0:1], vec[1:2]
    gain1, shift1, gain2, shift2 = vec[2:3], vec[3:4], vec[4:5], vec[5:6]

    @pl.when(i < tiles)
    def _():
        t = i
        slot = lax.rem(t, 3)
        copy(0, t).wait()
        keep = valid[0, :, :1]
        att = part[...].astype(F32) + got1[span(t)].astype(F32) + bias_out
        r1 = tok[...].astype(F32) + att
        centred = r1 - mean_last(r1)
        inverse = lax.rsqrt(mean_last(centred * centred) + LN_EPS)
        normal = centred * inverse
        normal1[slot] = normal
        inv1[slot] = jnp.broadcast_to(inverse, (blk, LANES))
        low = (normal * gain1 + shift1).astype(BF)
        hid[...] = low
        sums[6:7] += fold(keep * r1 * r1)
        sums[7:8] += fold(keep * att * att)
        for c in range(0, hidden, chunk):
            u = nn(low, w_up[:, c : c + chunk]) + b_up[:, c : c + chunk]
            both, gauss = erf_parts(u)
            act[:, c : c + chunk] = (0.5 * u * both).astype(BF)
            slope[lax.rem(t, 2), :, c : c + chunk] = (
                0.5 * both + u * gauss * INV_ROOT_TWO_PI
            ).astype(BF)
        send2[span(t)] = nn(act[...], w_down[...]).astype(BF)
        copy(1, t).start()

    @pl.when((i >= 1) & (i <= tiles))
    def _():
        t = i - 1
        copy(1, t).wait()
        keep = valid[1, :, :1]
        feed = send2[span(t)].astype(F32) + got2[span(t)].astype(F32) + bias_down
        r2 = normal1[lax.rem(t, 3)] * gain1 + shift1 + feed
        centred = r2 - mean_last(r2)
        inverse = lax.rsqrt(mean_last(centred * centred) + LN_EPS)
        normal = centred * inverse
        out[...] = (normal * gain2 + shift2).astype(BF)
        g = cot[...].astype(F32) * keep
        gr = norm_back(g, normal, inverse, gain2)
        grad2[lax.rem(t, 2)] = gr
        sums[1:2] += fold(gr)
        sums[4:5] += fold(g * normal)
        sums[5:6] += fold(g)
        sums[8:9] += fold(keep * feed * feed)
        low = gr.astype(BF)
        gfeed[...] = low
        for c in range(0, hidden, chunk):
            gu = nt(low, w_down[c : c + chunk]) * slope[lax.rem(t, 2), :, c : c + chunk].astype(F32)
            up_sum[0:1, c : c + chunk] += fold(gu)
            gpre[:, c : c + chunk] = gu.astype(BF)
        send3[span(t)] = nt(gpre[...], w_up[...]).astype(BF)
        copy(2, t).start()

    @pl.when(i >= 2)
    def _():
        t = i - 2
        slot = lax.rem(t, 3)
        copy(2, t).wait()
        gh = (
            grad2[lax.rem(t, 2)]
            + send3[span(t)].astype(F32)
            + got3[span(t)].astype(F32)
        )
        normal = normal1[slot]
        gr = norm_back(gh, normal, inv1[slot][:, :1], gain1)
        sums[0:1] += fold(gr)
        sums[2:3] += fold(gh * normal)
        sums[3:4] += fold(gh)
        r1_grad[...] = gr
        gattn[...] = gr.astype(BF)


def feed(tok, cot, valid, part, w_up, w_down, b_up, vec, blk=256):
    count, width = tok.shape
    hidden = w_up.shape[1]
    tiles = count // blk
    lag = lambda n: (lambda i: (jnp.clip(i - n, 0, tiles - 1), 0))
    whole = lambda shape: pl.BlockSpec(shape, lambda i: (0,) * len(shape))
    wide = lambda n: pl.BlockSpec((blk, width), lag(n))
    deep = lambda n: pl.BlockSpec((blk, hidden), lag(n))
    return pl.pallas_call(
        partial(feed_kernel_entry, tiles=tiles, blk=blk),
        grid=(tiles + 2,),
        in_specs=[
            wide(0),
            wide(1),
            pl.BlockSpec((blk, LANES), lag(0)),
            pl.BlockSpec((blk, LANES), lag(1)),
            wide(0),
            pl.BlockSpec(memory_space=pl.ANY),
            whole((width, hidden)),
            whole((hidden, width)),
            whole((1, hidden)),
            whole((8, width)),
        ],
        out_specs=[
            wide(1), wide(2), wide(2), deep(0), wide(0), wide(1), deep(1),
            whole((16, width)), whole((8, hidden)),
        ],
        out_shape=[
            jax.ShapeDtypeStruct((count, width), BF),
            jax.ShapeDtypeStruct((count, width), F32),
            jax.ShapeDtypeStruct((count, width), BF),
            jax.ShapeDtypeStruct((count, hidden), BF),
            jax.ShapeDtypeStruct((count, width), BF),
            jax.ShapeDtypeStruct((count, width), BF),
            jax.ShapeDtypeStruct((count, hidden), BF),
            jax.ShapeDtypeStruct((16, width), F32),
            jax.ShapeDtypeStruct((8, hidden), F32),
        ],
        scratch_shapes=[
            *[pltpu.VMEM((count, width), BF) for _ in range(5)],
            pltpu.VMEM((3, blk, width), F32),
            pltpu.VMEM((3, blk, LANES), F32),
            pltpu.VMEM((2, blk, width), F32),
            pltpu.VMEM((2, blk, hidden), BF),
            pltpu.SemaphoreType.DMA((3, tiles)),
            pltpu.SemaphoreType.DMA((3, tiles)),
        ],
        compiler_params=params(collective_id=1, has_side_effects=True),
        name="feed",
    )(tok, cot, valid, valid, part, part, w_up, w_down, b_up, vec)


class Both:
    def __init__(self, *refs):
        self.refs = refs

    def __getitem__(self, key):
        return self.refs[key[0]][key[1:]]


def feed_kernel_entry(tok, cot, valid0, valid1, *rest, tiles, blk):
    feed_kernel(tok, cot, Both(valid0, valid1), *rest, tiles=tiles, blk=blk)


def body(
    tokens,
    cotangent,
    pair_lengths,
    mat_master,
    mat_left,
    mat_right,
    root_left,
    root_right,
    vec_master,
    vec_second,
):
    width = tokens.shape[1]
    half = width // 2
    row_count, pair_count = pair_lengths.shape
    seq = tokens.shape[0] // row_count
    edge = mat_master.shape[-1]
    own_index = lax.axis_index("tensor")
    local = mat_master.astype(BF).reshape(3, -1, edge, edge)
    blocks = lax.all_gather(local, "dp", axis=1, tiled=True)
    kind_count = blocks.shape[1]
    quarter = kind_count // 4
    grid_model = width // edge
    grid_half = half // edge
    grid_hidden = kind_count // grid_model
    w_project = (
        blocks[0, : 3 * quarter]
        .reshape(3, grid_model, grid_half, edge, edge)
        .transpose(1, 3, 0, 2, 4)
        .reshape(width, 3 * half)
    )
    w_out = unblock(blocks[0, 3 * quarter :], grid_half, grid_model)
    w_up = unblock(blocks[1], grid_model, grid_hidden)
    w_down = unblock(blocks[2], grid_hidden, grid_model)
    shard = vec_master.shape[0]
    every = lax.all_gather(vec_master, ("dp", "tensor"), axis=0, tiled=True)
    halves = every.reshape(-1, 2, shard).transpose(1, 0, 2).reshape(2, 12, half)
    own = lax.dynamic_index_in_dim(halves, own_index, 0, keepdims=False)
    shared = jnp.concatenate([halves[0, 6:], halves[1, 6:]], axis=1)
    bias_up = own[2:6].reshape(1, -1)
    bias_qkv = jnp.concatenate([own[0], jnp.zeros((half,), F32), own[1]])[None]

    place = lax.broadcasted_iota(jnp.int32, (row_count, seq, pair_count), 1)
    upto = jnp.tril(jnp.ones((pair_count, pair_count), jnp.int32))
    ends = jnp.sum(pair_lengths[:, None, :] * upto[None], axis=-1)
    pairs = jnp.sum((place >= ends[:, None, :]).astype(jnp.int32), axis=-1)
    ids = lax.broadcasted_iota(jnp.int32, (row_count, seq, LANES), 2)
    same = pairs[:, :, None] == ids
    hot = same.astype(BF)
    cold = jnp.where(same & (ids < pair_count), 0.0, -BIG).astype(BF)
    keep = (pairs < pair_count).astype(F32).reshape(-1)
    valid = jnp.broadcast_to(keep[:, None], (keep.shape[0], LANES))

    qkv, ctx, lse, part = attn_fwd(tokens, w_project, w_out, bias_qkv, hot, cold, row_count, seq)
    vec_rows = jnp.concatenate([shared, jnp.zeros((2, width), F32)])
    block_out, gr1, gattn, act, hid, gfeed, gpre, sums, up_sum = feed(
        tokens, cotangent, valid, part, w_up, w_down, bias_up, vec_rows
    )
    grad_down = tn(act, gfeed).astype(BF)
    grad_up = tn(hid, gpre).astype(BF)
    gqkv, bias_sums, part_in = attn_bwd(
        gattn, qkv, ctx, lse, w_project, w_out, hot, cold, row_count, seq
    )
    grad_out_weight = tn(ctx, gattn).astype(BF)
    grad_project = tn(tokens, gqkv).astype(BF)
    swap = [(0, 1), (1, 0)]
    input_grad = gr1 + part_in.astype(F32) + lax.ppermute(part_in, "tensor", swap).astype(F32)

    squares, count = lax.psum((jnp.sum(sums[6:9], axis=1), jnp.sum(keep)), "dp")
    stream_rms = jnp.sqrt(squares / (count * width))

    project_blocks = (
        grad_project.reshape(grid_model, edge, 3, grid_half, edge)
        .transpose(2, 0, 3, 1, 4)
        .reshape(3 * quarter, edge, edge)
    )
    attention_blocks = jnp.concatenate([project_blocks, to_blocks(grad_out_weight, edge)], axis=0)
    feed_blocks = jnp.stack([to_blocks(grad_up, edge), to_blocks(grad_down, edge)])
    bias_pair = jnp.sum(bias_sums, axis=0)
    shared_sums = lax.dynamic_slice_in_dim(sums[:6], own_index * half, half, axis=1)
    vec_local = jnp.concatenate([bias_pair[:2].reshape(-1), up_sum[0], shared_sums.reshape(-1)])
    owned = lax.psum_scatter(
        jnp.concatenate([attention_blocks[None], feed_blocks], axis=0),
        "dp",
        scatter_dimension=1,
        tiled=True,
    )
    vec_grads = lax.psum_scatter(vec_local, "dp", scatter_dimension=0, tiled=True)
    mat_grads = owned.astype(F32).reshape(-1, edge, edge)
    left_new = DECAY * mat_left + (1.0 - DECAY) * jnp.einsum("bij,bkj->bik", mat_grads, mat_grads)
    right_new = DECAY * mat_right + (1.0 - DECAY) * jnp.einsum("bji,bjk->bik", mat_grads, mat_grads)
    turned = jnp.einsum("bij,bjk->bik", root_left, mat_grads)
    turned = jnp.einsum("bij,bjk->bik", turned, root_right)
    mat_new = mat_master - STEP_RATE * turned
    second_new = DECAY * vec_second + (1.0 - DECAY) * vec_grads * vec_grads
    vec_new = vec_master - VEC_RATE * vec_grads / (jnp.sqrt(second_new) + VEC_EPS)
    return (
        block_out,
        input_grad,
        mat_grads,
        left_new,
        right_new,
        mat_new,
        vec_grads,
        second_new,
        vec_new,
        stream_rms,
    )


def solution(mesh):
    blocks = P(("dp", "tensor"), None, None)
    rows = P("dp", None)
    entries = P(("dp", "tensor"))
    return jax.shard_map(
        body,
        mesh=mesh,
        in_specs=(rows, rows, rows, *[blocks] * 5, entries, entries),
        out_specs=(rows, rows, *[blocks] * 4, entries, entries, entries, P()),
        check_vma=False,
    )
```

```python
from functools import partial
import math

import jax
import jax.numpy as jnp
from jax import lax
from jax.experimental import pallas as pl
from jax.experimental.pallas import tpu as pltpu
from jax.sharding import PartitionSpec as P

HD = 64
LN_EPS = 1e-12
BIG = 1e30
FLOOR = -1e29
DECAY = 0.5
STEP_RATE = 1.0
VEC_RATE = 0.1
VEC_EPS = 1e-08
INV_ROOT_TWO = 1.0 / math.sqrt(2.0)
INV_ROOT_TWO_PI = 1.0 / math.sqrt(2.0 * math.pi)
BF = jnp.bfloat16
F32 = jnp.float32
LANES = 128
VMEM_LIMIT = 60 * 2**20
MESH = pl.DeviceIdType.MESH


def nn(a, b):
    return lax.dot_general(a, b, (((1,), (0,)), ((), ())), preferred_element_type=F32)


def nt(a, b):
    return lax.dot_general(a, b, (((1,), (1,)), ((), ())), preferred_element_type=F32)


def tn(a, b):
    return lax.dot_general(a, b, (((0,), (0,)), ((), ())), preferred_element_type=F32)


def unblock(blocks, grid_rows, grid_cols):
    edge = blocks.shape[-1]
    return (
        blocks.reshape(grid_rows, grid_cols, edge, edge)
        .transpose(0, 2, 1, 3)
        .reshape(grid_rows * edge, grid_cols * edge)
    )


def to_blocks(matrix, edge):
    grid_rows = matrix.shape[0] // edge
    grid_cols = matrix.shape[1] // edge
    return (
        matrix.reshape(grid_rows, edge, grid_cols, edge)
        .transpose(0, 2, 1, 3)
        .reshape(grid_rows * grid_cols, edge, edge)
    )


def erf_parts(u):
    z = jnp.abs(u) * INV_ROOT_TWO
    gauss = jnp.exp(-z * z)
    t = 1.0 / (1.0 + 0.3275911 * z)
    poly = t * (
        0.254829592
        + t * (-0.284496736 + t * (1.421413741 + t * (-1.453152027 + t * 1.061405429)))
    )
    tail = poly * gauss
    return jnp.where(u >= 0.0, 2.0 - tail, tail), gauss


def params(**kw):
    return pltpu.CompilerParams(vmem_limit_bytes=VMEM_LIMIT, **kw)


def low_lanes(shape):
    return lax.broadcasted_iota(jnp.int32, shape, 1) < HD


def attn_fwd_kernel(
    tok, w_qkv, w_out, bias, hot, cold, qkv, ctx, lse, part, *, half, seq, blk
):
    heads = half // HD
    qkv[...] = (nn(tok[...], w_qkv[...]) + bias[...]).astype(BF)
    low = low_lanes((blk, LANES))
    lane = lax.broadcasted_iota(jnp.int32, (blk, LANES), 1)

    def step(index, carry):
        rows = pl.ds(pl.multiple_of(index * blk, blk), blk)
        hot_blk = hot[0, rows, :]
        stats = jnp.zeros((blk, LANES), F32)
        for pair in range(heads // 2):
            cols = pl.ds(pair * LANES, LANES)
            q_pair = qkv[rows, cols] * jnp.asarray(HD**-0.5, BF)
            k_aug = jnp.concatenate(
                [qkv[:, pl.ds(half + pair * LANES, LANES)], cold[0]], axis=1
            )
            v_pair = qkv[:, pl.ds(2 * half + pair * LANES, LANES)]
            outs = []
            for side in range(2):
                own = low if side == 0 else jnp.logical_not(low)
                q_aug = jnp.concatenate([jnp.where(own, q_pair, 0), hot_blk], axis=1)
                s = nt(q_aug, k_aug)
                top = jnp.maximum(jnp.max(s, axis=1, keepdims=True), FLOOR)
                e = jnp.exp(s - top)
                total = jnp.maximum(jnp.sum(e, axis=1, keepdims=True), 0.5)
                outs.append(nn(e.astype(BF), v_pair) / total)
                stats = jnp.where(lane == 2 * pair + side, top + jnp.log(total), stats)
            ctx[rows, cols] = jnp.where(low, outs[0], outs[1]).astype(BF)
        lse[0, :, rows] = stats.T[: lse.shape[1]]
        return carry

    lax.fori_loop(0, seq // blk, step, 0)
    part[...] = nn(ctx[...], w_out[...]).astype(BF)


def attn_fwd(tok, w_qkv, w_out, bias, hot, cold, rows, seq):
    width = tok.shape[1]
    half = width // 2
    stat_rows = -(-(half // HD) // 8) * 8
    whole = lambda shape: pl.BlockSpec(shape, lambda r: (0,) * len(shape))
    return pl.pallas_call(
        partial(attn_fwd_kernel, half=half, seq=seq, blk=256),
        grid=(rows,),
        in_specs=[
            pl.BlockSpec((seq, width), lambda r: (r, 0)),
            whole((width, 3 * half)),
            whole((half, width)),
            whole((1, 3 * half)),
            pl.BlockSpec((1, seq, LANES), lambda r: (r, 0, 0)),
            pl.BlockSpec((1, seq, LANES), lambda r: (r, 0, 0)),
        ],
        out_specs=[
            pl.BlockSpec((seq, 3 * half), lambda r: (r, 0)),
            pl.BlockSpec((seq, half), lambda r: (r, 0)),
            pl.BlockSpec((1, stat_rows, seq), lambda r: (r, 0, 0)),
            pl.BlockSpec((seq, width), lambda r: (r, 0)),
        ],
        out_shape=[
            jax.ShapeDtypeStruct((rows * seq, 3 * half), BF),
            jax.ShapeDtypeStruct((rows * seq, half), BF),
            jax.ShapeDtypeStruct((rows, stat_rows, seq), F32),
            jax.ShapeDtypeStruct((rows * seq, width), BF),
        ],
        compiler_params=params(),
        name="attn_fwd",
    )(tok, w_qkv, w_out, bias, hot, cold)


def attn_bwd_kernel(
    gattn, qkv, ctx, lse, w_qkv, w_out, hot, cold, gqkv, sums, part, gctx, centre, dk, dv,
    *, half, seq, blk,
):
    heads = half // HD
    g = nt(gattn[...], w_out[...])
    gctx[...] = g.astype(BF)
    prod = gctx[...].astype(F32) * ctx[...].astype(F32)
    picks = (
        lax.broadcasted_iota(jnp.int32, (8, half), 0)
        == lax.broadcasted_iota(jnp.int32, (8, half), 1) // HD
    ).astype(F32)
    centre[...] = lax.dot_general(
        picks, prod, (((1,), (1,)), ((), ())),
        preferred_element_type=F32, precision=lax.Precision.HIGHEST,
    )
    low = low_lanes((blk, LANES))
    scale = jnp.asarray(HD**-0.5, BF)
    for pair in range(heads // 2):
        cols = pl.ds(pair * LANES, LANES)
        dk[...] = jnp.zeros_like(dk)
        dv[...] = jnp.zeros_like(dv)

        def step(index, gq_sum):
            rows = pl.ds(pl.multiple_of(index * blk, blk), blk)
            hot_blk = hot[0, rows, :]
            q_pair = qkv[rows, cols] * scale
            g_pair = gctx[rows, cols]
            k_pair = qkv[:, pl.ds(half + pair * LANES, LANES)]
            k_aug = jnp.concatenate([k_pair, cold[0]], axis=1)
            v_pair = qkv[:, pl.ds(2 * half + pair * LANES, LANES)]
            outs = []
            dk_new = dk[...]
            dv_new = dv[...]
            for side in range(2):
                head = 2 * pair + side
                own = low if side == 0 else jnp.logical_not(low)
                q_own = jnp.where(own, q_pair, 0)
                g_own = jnp.where(own, g_pair, 0)
                s = nt(k_aug, jnp.concatenate([q_own, hot_blk], axis=1))
                p = jnp.exp(s - lse[0, pl.ds(head, 1), rows])
                gp = nt(v_pair, g_own)
                gs = (p * (gp - centre[pl.ds(head, 1), rows])).astype(BF)
                dv_new = dv_new + nn(p.astype(BF), g_own)
                dk_new = dk_new + nn(gs, q_own)
                outs.append(tn(gs, k_pair))
            dk[...] = dk_new
            dv[...] = dv_new
            gq = jnp.where(low, outs[0], outs[1]) * HD**-0.5
            gqkv[rows, cols] = gq.astype(BF)
            return gq_sum + jnp.sum(gq, axis=0, keepdims=True)

        gq_sum = lax.fori_loop(0, seq // blk, step, jnp.zeros((1, LANES), F32))
        gqkv[:, pl.ds(half + pair * LANES, LANES)] = dk[...].astype(BF)
        gqkv[:, pl.ds(2 * half + pair * LANES, LANES)] = dv[...].astype(BF)
        sums[0, 0:1, cols] = gq_sum
        sums[0, 1:2, cols] = jnp.sum(dv[...], axis=0, keepdims=True)
    part[...] = nt(gqkv[...], w_qkv[...]).astype(BF)


def attn_bwd(gattn, qkv, ctx, lse, w_qkv, w_out, hot, cold, rows, seq):
    width = gattn.shape[1]
    half = width // 2
    whole = lambda shape: pl.BlockSpec(shape, lambda r: (0,) * len(shape))
    return pl.pallas_call(
        partial(attn_bwd_kernel, half=half, seq=seq, blk=256),
        grid=(rows,),
        in_specs=[
            pl.BlockSpec((seq, width), lambda r: (r, 0)),
            pl.BlockSpec((seq, 3 * half), lambda r: (r, 0)),
            pl.BlockSpec((seq, half), lambda r: (r, 0)),
            pl.BlockSpec((1, lse.shape[1], seq), lambda r: (r, 0, 0)),
            whole((width, 3 * half)),
            whole((half, width)),
            pl.BlockSpec((1, seq, LANES), lambda r: (r, 0, 0)),
            pl.BlockSpec((1, seq, LANES), lambda r: (r, 0, 0)),
        ],
        out_specs=[
            pl.BlockSpec((seq, 3 * half), lambda r: (r, 0)),
            pl.BlockSpec((1, 8, half), lambda r: (r, 0, 0)),
            pl.BlockSpec((seq, width), lambda r: (r, 0)),
        ],
        out_shape=[
            jax.ShapeDtypeStruct((rows * seq, 3 * half), BF),
            jax.ShapeDtypeStruct((rows, 8, half), F32),
            jax.ShapeDtypeStruct((rows * seq, width), BF),
        ],
        scratch_shapes=[
            pltpu.VMEM((seq, half), BF),
            pltpu.VMEM((8, seq), F32),
            pltpu.VMEM((seq, LANES), F32),
            pltpu.VMEM((seq, LANES), F32),
        ],
        compiler_params=params(),
        name="attn_bwd",
    )(gattn, qkv, ctx, lse, w_qkv, w_out, hot, cold)


def mean_last(x):
    return jnp.mean(x, axis=-1, keepdims=True)


def norm_back(grad, normal, inverse, gain):
    scaled = grad * gain
    return inverse * (scaled - mean_last(scaled) - normal * mean_last(scaled * normal))


def fold(x):
    return jnp.sum(x, axis=0, keepdims=True)


def feed_kernel(
    tok, cot, valid, part, part_all, w_up, w_down, b_up, vec,
    out, r1_grad, gattn, act, hid, gfeed, gpre, sums, up_sum,
    got1, send2, got2, send3, got3, normal1, inv1, grad2, slope, send_sem, recv_sem,
    *, tiles, blk,
):
    i = pl.program_id(0)
    other = 1 - lax.axis_index("tensor")
    width = tok.shape[1]
    hidden = w_down.shape[0]
    chunk = width

    def span(t):
        return pl.ds(pl.multiple_of(t * blk, blk), blk)

    def copy(stage, t):
        src = (part_all, send2, send3)[stage]
        dst = (got1, got2, got3)[stage]
        return pltpu.make_async_remote_copy(
            src_ref=src.at[span(t)],
            dst_ref=dst.at[span(t)],
            send_sem=send_sem.at[stage, t],
            recv_sem=recv_sem.at[stage, t],
            device_id={"tensor": other},
            device_id_type=MESH,
        )

    @pl.when(i == 0)
    def _():
        barrier = pltpu.get_barrier_semaphore()
        pl.semaphore_signal(barrier, inc=1, device_id={"tensor": other}, device_id_type=MESH)
        pl.semaphore_wait(barrier, 1)
        for t in range(tiles):
            copy(0, t).start()
        sums[...] = jnp.zeros_like(sums)
        up_sum[...] = jnp.zeros_like(up_sum)

    bias_out, bias_down = vec[0:1], vec[1:2]
    gain1, shift1, gain2, shift2 = vec[2:3], vec[3:4], vec[4:5], vec[5:6]

    @pl.when(i < tiles)
    def _():
        t = i
        slot = lax.rem(t, 3)
        copy(0, t).wait()
        keep = valid[0, :, :1]
        att = part[...].astype(F32) + got1[span(t)].astype(F32) + bias_out
        r1 = tok[...].astype(F32) + att
        centred = r1 - mean_last(r1)
        inverse = lax.rsqrt(mean_last(centred * centred) + LN_EPS)
        normal = centred * inverse
        normal1[slot] = normal
        inv1[slot] = jnp.broadcast_to(inverse, (blk, LANES))
        low = (normal * gain1 + shift1).astype(BF)
        hid[...] = low
        sums[6:7] += fold(keep * r1 * r1)
        sums[7:8] += fold(keep * att * att)
        for c in range(0, hidden, chunk):
            u = nn(low, w_up[c // chunk]) + b_up[:, c : c + chunk]
            both, gauss = erf_parts(u)
            act[:, c : c + chunk] = (0.5 * u * both).astype(BF)
            slope[lax.rem(t, 2), :, c : c + chunk] = (
                0.5 * both + u * gauss * INV_ROOT_TWO_PI
            ).astype(BF)
        send2[span(t)] = nn(act[...], w_down[...]).astype(BF)
        copy(1, t).start()

    @pl.when((i >= 1) & (i <= tiles))
    def _():
        t = i - 1
        copy(1, t).wait()
        keep = valid[1, :, :1]
        feed = send2[span(t)].astype(F32) + got2[span(t)].astype(F32) + bias_down
        r2 = normal1[lax.rem(t, 3)] * gain1 + shift1 + feed
        centred = r2 - mean_last(r2)
        inverse = lax.rsqrt(mean_last(centred * centred) + LN_EPS)
        normal = centred * inverse
        out[...] = (normal * gain2 + shift2).astype(BF)
        g = cot[...].astype(F32) * keep
        gr = norm_back(g, normal, inverse, gain2)
        grad2[lax.rem(t, 2)] = gr
        sums[1:2] += fold(gr)
        sums[4:5] += fold(g * normal)
        sums[5:6] += fold(g)
        sums[8:9] += fold(keep * feed * feed)
        low = gr.astype(BF)
        gfeed[...] = low
        for c in range(0, hidden, chunk):
            gu = nt(low, w_down[c : c + chunk]) * slope[lax.rem(t, 2), :, c : c + chunk].astype(F32)
            up_sum[0:1, c : c + chunk] += fold(gu)
            gpre[:, c : c + chunk] = gu.astype(BF)
        send3[span(t)] = (
            nt(gpre[:, :chunk], w_up[0]) + nt(gpre[:, chunk:], w_up[1])
        ).astype(BF)
        copy(2, t).start()

    @pl.when(i >= 2)
    def _():
        t = i - 2
        slot = lax.rem(t, 3)
        copy(2, t).wait()
        gh = (
            grad2[lax.rem(t, 2)]
            + send3[span(t)].astype(F32)
            + got3[span(t)].astype(F32)
        )
        normal = normal1[slot]
        gr = norm_back(gh, normal, inv1[slot][:, :1], gain1)
        sums[0:1] += fold(gr)
        sums[2:3] += fold(gh * normal)
        sums[3:4] += fold(gh)
        r1_grad[...] = gr
        gattn[...] = gr.astype(BF)


def feed(tok, cot, valid, part, w_up, w_down, b_up, vec, blk=256):
    count, width = tok.shape
    hidden = w_down.shape[0]
    tiles = count // blk
    lag = lambda n: (lambda i: (jnp.clip(i - n, 0, tiles - 1), 0))
    whole = lambda shape: pl.BlockSpec(shape, lambda i: (0,) * len(shape))
    wide = lambda n: pl.BlockSpec((blk, width), lag(n))
    deep = lambda n: pl.BlockSpec((blk, hidden), lag(n))
    return pl.pallas_call(
        partial(feed_kernel_entry, tiles=tiles, blk=blk),
        grid=(tiles + 2,),
        in_specs=[
            wide(0),
            wide(1),
            pl.BlockSpec((blk, LANES), lag(0)),
            pl.BlockSpec((blk, LANES), lag(1)),
            wide(0),
            pl.BlockSpec(memory_space=pl.ANY),
            whole(w_up.shape),
            whole((hidden, width)),
            whole((1, hidden)),
            whole((8, width)),
        ],
        out_specs=[
            wide(1), wide(2), wide(2), deep(0), wide(0), wide(1), deep(1),
            whole((16, width)), whole((8, hidden)),
        ],
        out_shape=[
            jax.ShapeDtypeStruct((count, width), BF),
            jax.ShapeDtypeStruct((count, width), F32),
            jax.ShapeDtypeStruct((count, width), BF),
            jax.ShapeDtypeStruct((count, hidden), BF),
            jax.ShapeDtypeStruct((count, width), BF),
            jax.ShapeDtypeStruct((count, width), BF),
            jax.ShapeDtypeStruct((count, hidden), BF),
            jax.ShapeDtypeStruct((16, width), F32),
            jax.ShapeDtypeStruct((8, hidden), F32),
        ],
        scratch_shapes=[
            *[pltpu.VMEM((count, width), BF) for _ in range(5)],
            pltpu.VMEM((3, blk, width), F32),
            pltpu.VMEM((3, blk, LANES), F32),
            pltpu.VMEM((2, blk, width), F32),
            pltpu.VMEM((2, blk, hidden), BF),
            pltpu.SemaphoreType.DMA((3, tiles)),
            pltpu.SemaphoreType.DMA((3, tiles)),
        ],
        compiler_params=params(collective_id=1, has_side_effects=True),
        name="feed",
    )(tok, cot, valid, valid, part, part, w_up, w_down, b_up, vec)


class Both:
    def __init__(self, *refs):
        self.refs = refs

    def __getitem__(self, key):
        return self.refs[key[0]][key[1:]]


def feed_kernel_entry(tok, cot, valid0, valid1, *rest, tiles, blk):
    feed_kernel(tok, cot, Both(valid0, valid1), *rest, tiles=tiles, blk=blk)


PLANE = 4
DEPTH = 4
UP, DOWN, ALONG_X, ALONG_Y = 0, 1, 2, 3


def where_am_i():
    dp = lax.axis_index("dp")
    return dp, dp // PLANE, lax.rem(dp, PLANE)


def flip(xy, bit):
    step = 1 if bit == ALONG_X else 2
    side = lax.rem(xy // step, 2)
    return xy + step - 2 * step * side


def toward(direction):
    dp, z, xy = where_am_i()
    if direction == UP:
        return dp + PLANE
    if direction == DOWN:
        return dp - PLANE
    return z * PLANE + flip(xy, direction)


def greet():
    dp, z, xy = where_am_i()
    barrier = pltpu.get_barrier_semaphore()
    other = 1 - lax.axis_index("tensor")

    def tell(device):
        pl.semaphore_signal(barrier, inc=1, device_id=device, device_id_type=MESH)

    tell({"tensor": other})
    tell({"dp": toward(ALONG_X)})
    tell({"dp": toward(ALONG_Y)})
    pl.when(z < DEPTH - 1)(lambda: tell({"dp": toward(UP)}))
    pl.when(z > 0)(lambda: tell({"dp": toward(DOWN)}))
    inner = jnp.logical_and(z < DEPTH - 1, z > 0)
    pl.semaphore_wait(barrier, jnp.where(inner, 5, 4))


class Gather:
    def __init__(self, kinds, send_sem, recv_sem):
        self.kinds = kinds
        self.send_sem, self.recv_sem = send_sem, recv_sem
        self.dp, self.z, self.xy = where_am_i()
        self.started = []

    def copy(self, c, direction, origin, part):
        place, first, rows = self.kinds[c]
        ref = place(origin)
        if part == 1:
            ref = ref.at[pl.ds(0, first)]
        if part == 2:
            ref = ref.at[pl.ds(first, rows - first)]
        slot = origin if part != 2 else DEPTH * PLANE + origin // PLANE
        lane = direction if part == 0 else direction + 2
        return pltpu.make_async_remote_copy(
            src_ref=ref,
            dst_ref=ref,
            send_sem=self.send_sem.at[c, lane, origin],
            recv_sem=self.recv_sem.at[c, slot],
            device_id={"dp": toward(direction)},
            device_id_type=MESH,
        )

    def send(self, ok, c, direction, origin, part=0):
        start = lambda: self.copy(c, direction, origin, part).start()
        start() if ok is None else pl.when(ok)(start)
        self.started.append((ok, c, direction, origin, part))

    def levels(self, k):
        if k == 0:
            return [(None, self.z)]
        below, above = self.z - k, self.z + k
        return [(below >= 0, below), (above < DEPTH, above)]

    def along(self, c, k):
        for ok, level in self.levels(k):
            origin = level * PLANE + self.xy
            up, down = self.z < DEPTH - 1, self.z > 0
            if k == 0:
                self.send(up, c, UP, origin)
                self.send(down, c, DOWN, origin)
            else:
                pl.when(ok)(lambda: self.copy(c, ALONG_X, origin, 0).wait_recv())
                from_below = level < self.z
                self.send(ok & from_below & up, c, UP, origin)
                self.send(ok & jnp.logical_not(from_below) & down, c, DOWN, origin)
            self.send(ok, c, ALONG_X, origin)
            self.send(ok, c, ALONG_Y, origin)

    def across(self, c, k):
        first, rows = self.kinds[c][1:]
        for ok, level in self.levels(k):
            for came, onward, part in ((ALONG_X, ALONG_Y, 1), (ALONG_Y, ALONG_X, 2)):
                origin = level * PLANE + flip(self.xy, came)
                wait = lambda came=came, origin=origin: self.copy(c, came, origin, 0).wait_recv()
                wait() if ok is None else pl.when(ok)(wait)
                if part == 1 or rows > first:
                    self.send(ok, c, onward, origin, part if rows > first else 3)

    def last(self, c):
        first, rows = self.kinds[c][1:]
        diag = flip(flip(self.xy, ALONG_X), ALONG_Y)
        for level in range(DEPTH):
            origin = level * PLANE + diag
            if rows > first:
                self.copy(c, ALONG_Y, origin, 1).wait_recv()
                self.copy(c, ALONG_X, origin, 2).wait_recv()
            else:
                self.copy(c, ALONG_Y, origin, 3).wait_recv()

    def sent(self):
        for ok, c, direction, origin, part in self.started:
            lane = max(direction, ALONG_X) if part else direction
            wait = lambda: self.copy(c, lane, origin, part).wait_send()
            wait() if ok is None else pl.when(ok)(wait)
        self.started = []


class Scatter:
    def __init__(self, kinds, bufs, send_sem, recv_sem):
        self.kinds, self.bufs = kinds, bufs
        self.send_sem, self.recv_sem = send_sem, recv_sem
        self.dp, self.z, self.xy = where_am_i()
        self.started = []

    def level(self, k):
        return jnp.where(self.z < DEPTH // 2, DEPTH - 1 - k, k)

    def copy(self, c, what, src, dst, direction, level):
        return pltpu.make_async_remote_copy(
            src_ref=src,
            dst_ref=dst,
            send_sem=self.send_sem.at[c, what, level],
            recv_sem=self.recv_sem.at[c, what, level],
            device_id={"dp": toward(direction)},
            device_id_type=MESH,
        )

    def term(self, c, column, level):
        return self.kinds[c][0](level * PLANE + column)

    def parts(self, c, what, level):
        place, first, rows, _ = self.kinds[c]
        got_a, got_b, got_x, got_y, got_up, got_down, put_x, put_y, put_z = self.bufs[c]
        diag = flip(flip(self.xy, ALONG_X), ALONG_Y)
        if what == 0:
            return self.term(c, diag, level).at[pl.ds(0, first)], got_a.at[level], ALONG_Y
        if what == 1:
            return self.term(c, diag, level).at[pl.ds(first, rows - first)], got_b.at[level], ALONG_X
        if what == 2:
            return put_x.at[level], got_x.at[level], ALONG_X
        if what == 3:
            return put_y.at[level], got_y.at[level], ALONG_Y
        if what == 4:
            return put_z.at[level], got_up.at[level], UP
        return put_z.at[level], got_down.at[level], DOWN

    def start(self, c, what, level):
        src, dst, direction = self.parts(c, what, level)
        self.copy(c, what, src, dst, direction, level).start()

    def wait(self, c, what, level, sent=False):
        src, dst, direction = self.parts(c, what, level)
        copy = self.copy(c, what, src, dst, ALONG_X, level)
        copy.wait_send() if sent else copy.wait_recv()

    def first(self, c, k):
        place, first, rows, _ = self.kinds[c]
        self.start(c, 0, self.level(k))
        if rows > first:
            self.start(c, 1, self.level(k))

    def second(self, c, k):
        place, first, rows, _ = self.kinds[c]
        level = self.level(k)
        got_a, got_b, _, _, _, _, put_x, put_y, _ = self.bufs[c]
        a, b = pl.ds(0, first), pl.ds(first, rows - first)
        own_x = self.term(c, flip(self.xy, ALONG_X), level)
        own_y = self.term(c, flip(self.xy, ALONG_Y), level)
        self.wait(c, 0, level)
        add = lambda p, q: (p.astype(F32) + q.astype(F32)).astype(put_x.dtype)
        put_x[level, a] = add(own_x[a], got_a[level])
        if rows > first:
            put_x[level, b] = own_x[b]
        self.start(c, 2, level)
        if rows > first:
            self.wait(c, 1, level)
            put_y[level, b] = add(own_y[b], got_b[level])
        put_y[level, a] = own_y[a]
        self.start(c, 3, level)

    def third(self, c, k):
        level = self.level(k)
        _, _, got_x, got_y, got_up, got_down, _, _, put_z = self.bufs[c]
        total = self.kinds[c][3]
        self.wait(c, 2, level)
        self.wait(c, 3, level)
        own = self.term(c, self.xy, level)
        here = own[...].astype(F32) + got_x[level].astype(F32) + got_y[level].astype(F32)

        @pl.when(level == self.z)
        def _():
            total[...] = here

        for what, beyond, more, got in (
            (4, level > self.z, self.z > 0, got_up),
            (5, level < self.z, self.z < DEPTH - 1, got_down),
        ):

            @pl.when(jnp.logical_and(beyond, jnp.logical_not(more)))
            def _():
                put_z[level] = here.astype(put_z.dtype)
                self.start(c, what, level)

            @pl.when(jnp.logical_and(beyond, more))
            def _():
                self.wait(c, what, level)
                put_z[level] = (here + got[level].astype(F32)).astype(put_z.dtype)
                self.start(c, what, level)

    def last(self, c):
        got_up, got_down = self.bufs[c][4:6]
        total = self.kinds[c][3]

        @pl.when(self.z > 0)
        def _():
            self.wait(c, 4, self.z)
            total[...] += got_up[self.z].astype(F32)

        @pl.when(self.z < DEPTH - 1)
        def _():
            self.wait(c, 5, self.z)
            total[...] += got_down[self.z].astype(F32)

    def sent(self, c):
        place, first, rows, _ = self.kinds[c]
        for level in range(DEPTH):
            self.wait(c, 0, level, True)
            if rows > first:
                self.wait(c, 1, level, True)
            self.wait(c, 2, level, True)
            self.wait(c, 3, level, True)
            pl.when(level > self.z)(lambda: self.wait(c, 4, level, True))
            pl.when(level < self.z)(lambda: self.wait(c, 5, level, True))


GATHER_SLOTS = DEPTH * PLANE + DEPTH
KINDS = 3


def gather_kernel(mat, vec, w0, w1, w2, vecs, send_sem, recv_sem, swap_sem, *, edge, per):
    half, width = w0.shape[2], w1.shape[2]
    dp, z, xy = where_am_i()
    own = lax.axis_index("tensor")
    wide = per * edge
    greet()

    def place0(d):
        return w0.at[d // PLANE, pl.ds(pl.multiple_of(lax.rem(d, PLANE) * 2 * edge, 2 * edge), 2 * edge)]

    def place1(d):
        return w1.at[lax.rem(d, 2), pl.ds(pl.multiple_of(d // 2 * edge, edge), edge)]

    def place2(d):
        return w2.at[pl.ds(pl.multiple_of(d * edge, edge), edge)]

    def place3(d):
        return vecs.at[own, d]

    gather = Gather(
        [
            (place3, vec.shape[0], vec.shape[0]),
            (place0, edge, 2 * edge),
            (place1, edge // 2, edge),
            (place2, edge // 2, edge),
        ],
        send_sem,
        recv_sem,
    )
    place3(dp)[...] = vec[...]
    gather.along(0, 0)
    mine0, mine1, mine2 = place0(dp), place1(dp), place2(dp)
    for j in range(per):
        at = pl.ds(j % (per // 2) * edge, edge)
        mine0[pl.ds(j // (per // 2) * edge, edge), at] = mat[j].astype(BF)
    gather.along(1, 0)
    for j in range(per):
        mine1[:, pl.ds(j * edge, edge)] = mat[per + j].astype(BF)
        mine2[:, pl.ds(j * edge, edge)] = mat[2 * per + j].astype(BF)
    for k in range(1, DEPTH):
        gather.along(0, k)
        gather.across(0, k - 1)
        gather.along(1, k)
        gather.across(1, k - 1)
    gather.across(0, DEPTH - 1)
    gather.across(1, DEPTH - 1)
    gather.along(2, 0)
    for k in range(1, DEPTH):
        gather.along(2, k)
        gather.across(2, k - 1)
    gather.across(2, DEPTH - 1)
    gather.along(3, 0)
    gather.last(0)
    swap = pltpu.make_async_remote_copy(
        src_ref=vecs.at[own],
        dst_ref=vecs.at[own],
        send_sem=swap_sem.at[0],
        recv_sem=swap_sem.at[1],
        device_id={"tensor": 1 - own},
        device_id_type=MESH,
    )
    swap.start()
    gather.last(1)
    gather.last(2)
    for k in range(1, DEPTH):
        gather.along(3, k)
        gather.across(3, k - 1)
    gather.across(3, DEPTH - 1)
    gather.last(3)
    gather.sent()
    swap.wait()


def gather_weights(mat, vec):
    per, edge = mat.shape[0] // KINDS, mat.shape[-1]
    wide = per * edge
    count = DEPTH * PLANE
    vmem = pl.BlockSpec(memory_space=pltpu.VMEM)
    return pl.pallas_call(
        partial(gather_kernel, edge=edge, per=per),
        in_specs=[vmem] * 2,
        out_specs=[vmem] * 4,
        out_shape=[
            jax.ShapeDtypeStruct((4, wide, wide // 2), BF),
            jax.ShapeDtypeStruct((2, wide, wide), BF),
            jax.ShapeDtypeStruct((2 * wide, wide), BF),
            jax.ShapeDtypeStruct((2, count, *vec.shape), F32),
        ],
        scratch_shapes=[
            pltpu.SemaphoreType.DMA((4, 6, count)),
            pltpu.SemaphoreType.DMA((4, GATHER_SLOTS)),
            pltpu.SemaphoreType.DMA((2,)),
        ],
        compiler_params=params(collective_id=2, has_side_effects=True),
        name="gather_weights",
    )(mat, vec)


SCATTER_BUFS = 9


def scatter_kernel(
    g0, g1, g2, gv, master, left, right, root_l, root_r,
    grads, left_new, right_new, mat_new, vec_total, total0, total1, *rest, edge, per,
):
    bufs, (send_sem, recv_sem) = rest[:-2], rest[-2:]
    bufs = [bufs[c * SCATTER_BUFS : (c + 1) * SCATTER_BUFS] for c in range(4)]

    def place0(d):
        return g0.at[d]

    def place1(d):
        return g1.at[lax.rem(d, 2), pl.ds(pl.multiple_of(d // 2 * edge, edge), edge)]

    def place2(d):
        return g2.at[pl.ds(pl.multiple_of(d * edge, edge), edge)]

    def place3(d):
        return gv.at[d]

    kinds = [
        (place3, gv.shape[1], gv.shape[1], vec_total),
        (place2, edge // 2, edge, total1),
        (place1, edge // 2, edge, total1),
        (place0, edge, 2 * edge, total0),
    ]
    scatter = Scatter(kinds, bufs, send_sem, recv_sem)
    greet()

    def block(number, grad):
        low = grad.astype(BF)
        grads[number] = grad
        left_new[number] = DECAY * left[number] + (1.0 - DECAY) * nt(low, low)
        right_new[number] = DECAY * right[number] + (1.0 - DECAY) * tn(low, low)
        turned = nn(root_l[number].astype(BF), low).astype(BF)
        mat_new[number] = master[number] - STEP_RATE * nn(turned, root_r[number].astype(BF))

    def finish(c):
        if c == 3:
            for j in range(per):
                block(j, total0[pl.ds(j // (per // 2) * edge, edge), pl.ds(j % (per // 2) * edge, edge)])
        else:
            base = (3 - c) * per
            for j in range(per):
                block(base + j, total1[:, pl.ds(j * edge, edge)])

    for c in range(4):
        for k in range(DEPTH):
            scatter.first(c, k)
        for k in range(DEPTH):
            scatter.second(c, k)
        if c > 0:
            for k in range(DEPTH):
                scatter.third(c - 1, k)
            scatter.last(c - 1)
            if c > 1:
                finish(c - 1)
    for k in range(DEPTH):
        scatter.third(3, k)
    scatter.last(3)
    finish(3)
    for c in range(4):
        scatter.sent(c)


def scatter_grads(g0, g1, g2, gv, master, left, right, root_l, root_r):
    per, edge = master.shape[0] // KINDS, master.shape[-1]
    wide = per * edge
    vmem = pl.BlockSpec(memory_space=pltpu.VMEM)
    rows = gv.shape[1]

    def bufs(first, full, cols, kind):
        a, b = (DEPTH, first, cols), (DEPTH, max(full - first, first), cols)
        f = (DEPTH, full, cols)
        return [pltpu.VMEM(s, kind) for s in (a, b, f, f, f, f, f, f, f)]

    return pl.pallas_call(
        partial(scatter_kernel, edge=edge, per=per),
        in_specs=[vmem] * 9,
        out_specs=[vmem] * 5,
        out_shape=[jax.ShapeDtypeStruct(master.shape, F32)] * 4
        + [jax.ShapeDtypeStruct(gv.shape[1:], F32)],
        scratch_shapes=[
            pltpu.VMEM((2 * edge, wide // 2), F32),
            pltpu.VMEM((edge, wide), F32),
            *bufs(rows, rows, gv.shape[2], F32),
            *bufs(edge // 2, edge, wide, BF),
            *bufs(edge // 2, edge, wide, BF),
            *bufs(edge, 2 * edge, wide // 2, BF),
            pltpu.SemaphoreType.DMA((4, 6, DEPTH)),
            pltpu.SemaphoreType.DMA((4, 6, DEPTH)),
        ],
        compiler_params=params(collective_id=3, has_side_effects=True),
        name="scatter_grads",
    )(g0, g1, g2, gv, master, left, right, root_l, root_r)


def far_weights(mat_master, vec_master, width):
    half = width // 2
    edge = mat_master.shape[-1]
    local = mat_master.astype(BF).reshape(KINDS, -1, edge, edge)
    blocks = lax.all_gather(local, "dp", axis=1, tiled=True)
    kind_count = blocks.shape[1]
    quarter = kind_count // 4
    grid_model = width // edge
    grid_half = half // edge
    grid_hidden = kind_count // grid_model
    w_project = (
        blocks[0, : 3 * quarter]
        .reshape(3, grid_model, grid_half, edge, edge)
        .transpose(1, 3, 0, 2, 4)
        .reshape(width, 3 * half)
    )
    w_out = unblock(blocks[0, 3 * quarter :], grid_half, grid_model)
    w_up = unblock(blocks[1], grid_model, grid_hidden).reshape(width, -1, width)
    w_down = unblock(blocks[2], grid_hidden, grid_model)
    shard = vec_master.shape[0]
    every = lax.all_gather(vec_master, ("dp", "tensor"), axis=0, tiled=True)
    halves = every.reshape(-1, 2, shard).transpose(1, 0, 2).reshape(2, 12, half)
    return w_project, w_out, w_up.transpose(1, 0, 2), w_down, halves


def near_weights(mat_master, vec_master, width):
    half = width // 2
    edge = mat_master.shape[-1]
    shard = vec_master.shape[0]
    rows = -(-shard // LANES)
    vec = jnp.pad(vec_master, (0, 8 * LANES - shard)).reshape(8, LANES)
    w0, w_up, w_down, vecs = gather_weights(mat_master, vec)
    halves = vecs[:, :, :rows].reshape(2, -1, rows * LANES)[:, :, :shard].reshape(2, 12, half)
    w_project = w0[:3].transpose(1, 0, 2).reshape(width, 3 * half)
    w_out = w0[3].reshape(-1, 2, edge, half).transpose(0, 2, 1, 3).reshape(half, width)
    return w_project, w_out, w_up, w_down, halves


def far_step(grads, state):
    grad_project, grad_out_weight, grad_up, grad_down, vec_local, sizes = grads
    mat_master, mat_left, mat_right, root_left, root_right = state
    edge = mat_master.shape[-1]
    width, half = grad_project.shape[0], grad_project.shape[1] // 3
    project_blocks = (
        grad_project.reshape(width // edge, edge, 3, half // edge, edge)
        .transpose(2, 0, 3, 1, 4)
        .reshape(-1, edge, edge)
    )
    attention_blocks = jnp.concatenate([project_blocks, to_blocks(grad_out_weight, edge)], axis=0)
    owned = lax.psum_scatter(
        jnp.stack([attention_blocks, to_blocks(grad_up, edge), to_blocks(grad_down, edge)]),
        "dp",
        scatter_dimension=1,
        tiled=True,
    )
    vec_grads = lax.psum_scatter(vec_local, "dp", scatter_dimension=0, tiled=True)
    mat_grads = owned.astype(F32).reshape(-1, edge, edge)
    left_new = DECAY * mat_left + (1.0 - DECAY) * jnp.einsum("bij,bkj->bik", mat_grads, mat_grads)
    right_new = DECAY * mat_right + (1.0 - DECAY) * jnp.einsum("bji,bjk->bik", mat_grads, mat_grads)
    turned = jnp.einsum("bij,bjk->bik", root_left, mat_grads)
    turned = jnp.einsum("bij,bjk->bik", turned, root_right)
    mat_new = mat_master - STEP_RATE * turned
    return mat_grads, left_new, right_new, mat_new, vec_grads, lax.psum(sizes, "dp")


def near_step(grads, state):
    grad_project, grad_out_weight, grad_up, grad_down, vec_local, sizes = grads
    edge = state[0].shape[-1]
    width, half = grad_project.shape[0], grad_project.shape[1] // 3
    count = DEPTH * PLANE
    shard = vec_local.shape[0] // count
    room = 8 * LANES
    project = grad_project.reshape(PLANE, 2 * edge, 3, half).transpose(2, 0, 1, 3)
    out = grad_out_weight.reshape(PLANE, edge, 2, half).transpose(0, 2, 1, 3)
    g0 = jnp.concatenate(
        [project.reshape(3 * PLANE, 2 * edge, half), out.reshape(PLANE, 2 * edge, half)]
    )
    g1 = grad_up.reshape(width, 2, width).transpose(1, 0, 2)
    spread = jnp.broadcast_to(sizes[None], (count, sizes.shape[0]))
    gv = jnp.concatenate([vec_local.reshape(count, shard), spread], axis=1)
    gv = jnp.pad(gv, ((0, 0), (0, room - gv.shape[1]))).reshape(count, 8, LANES)
    *mats, vec_total = scatter_grads(g0, g1, grad_down, gv, *state)
    flat = vec_total.reshape(-1)
    return *mats, flat[:shard], flat[shard : shard + sizes.shape[0]]


def body(
    tokens,
    cotangent,
    pair_lengths,
    mat_master,
    mat_left,
    mat_right,
    root_left,
    root_right,
    vec_master,
    vec_second,
):
    width = tokens.shape[1]
    half = width // 2
    row_count, pair_count = pair_lengths.shape
    seq = tokens.shape[0] // row_count
    edge = mat_master.shape[-1]
    own_index = lax.axis_index("tensor")
    shard = vec_master.shape[0]
    fast = lax.axis_size("dp") == DEPTH * PLANE and mat_master.shape[0] == KINDS * width // edge
    weights = near_weights if fast else far_weights
    w_project, w_out, w_up, w_down, halves = weights(mat_master, vec_master, width)
    own = lax.dynamic_index_in_dim(halves, own_index, 0, keepdims=False)
    shared = jnp.concatenate([halves[0, 6:], halves[1, 6:]], axis=1)
    bias_up = own[2:6].reshape(1, -1)
    bias_qkv = jnp.concatenate([own[0], jnp.zeros((half,), F32), own[1]])[None]

    place = lax.broadcasted_iota(jnp.int32, (row_count, seq, pair_count), 1)
    upto = jnp.tril(jnp.ones((pair_count, pair_count), jnp.int32))
    ends = jnp.sum(pair_lengths[:, None, :] * upto[None], axis=-1)
    pairs = jnp.sum((place >= ends[:, None, :]).astype(jnp.int32), axis=-1)
    ids = lax.broadcasted_iota(jnp.int32, (row_count, seq, LANES), 2)
    same = pairs[:, :, None] == ids
    hot = same.astype(BF)
    cold = jnp.where(same & (ids < pair_count), 0.0, -BIG).astype(BF)
    keep = (pairs < pair_count).astype(F32).reshape(-1)
    valid = jnp.broadcast_to(keep[:, None], (keep.shape[0], LANES))

    qkv, ctx, lse, part = attn_fwd(tokens, w_project, w_out, bias_qkv, hot, cold, row_count, seq)
    vec_rows = jnp.concatenate([shared, jnp.zeros((2, width), F32)])
    block_out, gr1, gattn, act, hid, gfeed, gpre, sums, up_sum = feed(
        tokens, cotangent, valid, part, w_up, w_down, bias_up, vec_rows
    )
    grad_down = tn(act, gfeed).astype(BF)
    grad_up = tn(hid, gpre).astype(BF)
    gqkv, bias_sums, part_in = attn_bwd(
        gattn, qkv, ctx, lse, w_project, w_out, hot, cold, row_count, seq
    )
    grad_out_weight = tn(ctx, gattn).astype(BF)
    grad_project = tn(tokens, gqkv).astype(BF)
    swap = [(0, 1), (1, 0)]
    input_grad = gr1 + part_in.astype(F32) + lax.ppermute(part_in, "tensor", swap).astype(F32)

    sizes = jnp.concatenate([jnp.sum(sums[6:9], axis=1), jnp.sum(keep)[None]])
    bias_pair = jnp.sum(bias_sums, axis=0)
    shared_sums = lax.dynamic_slice_in_dim(sums[:6], own_index * half, half, axis=1)
    vec_local = jnp.concatenate([bias_pair[:2].reshape(-1), up_sum[0], shared_sums.reshape(-1)])
    step = near_step if fast else far_step
    mat_grads, left_new, right_new, mat_new, vec_grads, sizes = step(
        (grad_project, grad_out_weight, grad_up, grad_down, vec_local, sizes),
        (mat_master, mat_left, mat_right, root_left, root_right),
    )
    stream_rms = jnp.sqrt(sizes[:3] / (sizes[3] * width))
    second_new = DECAY * vec_second + (1.0 - DECAY) * vec_grads * vec_grads
    vec_new = vec_master - VEC_RATE * vec_grads / (jnp.sqrt(second_new) + VEC_EPS)
    return (
        block_out,
        input_grad,
        mat_grads,
        left_new,
        right_new,
        mat_new,
        vec_grads,
        second_new,
        vec_new,
        stream_rms,
    )


def solution(mesh):
    blocks = P(("dp", "tensor"), None, None)
    rows = P("dp", None)
    entries = P(("dp", "tensor"))
    return jax.shard_map(
        body,
        mesh=mesh,
        in_specs=(rows, rows, rows, *[blocks] * 5, entries, entries),
        out_specs=(rows, rows, *[blocks] * 4, entries, entries, entries, P()),
        check_vma=False,
    )
```

```python
from functools import partial
import math

import jax
import jax.numpy as jnp
from jax import lax
from jax.experimental import pallas as pl
from jax.experimental.pallas import tpu as pltpu
from jax.sharding import PartitionSpec as P

HD = 64
LN_EPS = 1e-12
BIG = 1e30
FLOOR = -1e29
DECAY = 0.5
STEP_RATE = 1.0
VEC_RATE = 0.1
VEC_EPS = 1e-08
INV_ROOT_TWO = 1.0 / math.sqrt(2.0)
INV_ROOT_TWO_PI = 1.0 / math.sqrt(2.0 * math.pi)
BF = jnp.bfloat16
F32 = jnp.float32
LANES = 128
VMEM_LIMIT = 60 * 2**20
MESH = pl.DeviceIdType.MESH


def nn(a, b):
    return lax.dot_general(a, b, (((1,), (0,)), ((), ())), preferred_element_type=F32)


def nt(a, b):
    return lax.dot_general(a, b, (((1,), (1,)), ((), ())), preferred_element_type=F32)


def tn(a, b):
    return lax.dot_general(a, b, (((0,), (0,)), ((), ())), preferred_element_type=F32)


def unblock(blocks, grid_rows, grid_cols):
    edge = blocks.shape[-1]
    return (
        blocks.reshape(grid_rows, grid_cols, edge, edge)
        .transpose(0, 2, 1, 3)
        .reshape(grid_rows * edge, grid_cols * edge)
    )


def to_blocks(matrix, edge):
    grid_rows = matrix.shape[0] // edge
    grid_cols = matrix.shape[1] // edge
    return (
        matrix.reshape(grid_rows, edge, grid_cols, edge)
        .transpose(0, 2, 1, 3)
        .reshape(grid_rows * grid_cols, edge, edge)
    )


def erf_parts(u):
    z = jnp.abs(u) * INV_ROOT_TWO
    gauss = jnp.exp(-z * z)
    t = 1.0 / (1.0 + 0.3275911 * z)
    poly = t * (
        0.254829592
        + t * (-0.284496736 + t * (1.421413741 + t * (-1.453152027 + t * 1.061405429)))
    )
    tail = poly * gauss
    return jnp.where(u >= 0.0, 2.0 - tail, tail), gauss


def params(**kw):
    return pltpu.CompilerParams(vmem_limit_bytes=VMEM_LIMIT, **kw)


def low_lanes(shape):
    return lax.broadcasted_iota(jnp.int32, shape, 1) < HD


def attend(qkv, ctx, hot, cold, rows, half, between=None):
    blk = hot.shape[0]
    low = low_lanes((blk, LANES))
    lane = lax.broadcasted_iota(jnp.int32, (blk, LANES), 1)
    stats = jnp.zeros((blk, LANES), F32)
    for pair in range(half // LANES):
        if between is not None:
            between(pair)
        cols = pl.ds(pair * LANES, LANES)
        q_pair = qkv[rows, cols] * jnp.asarray(HD**-0.5, BF)
        k_aug = jnp.concatenate([qkv[:, pl.ds(half + pair * LANES, LANES)], cold], axis=1)
        v_pair = qkv[:, pl.ds(2 * half + pair * LANES, LANES)]
        outs = []
        for side in range(2):
            own = low if side == 0 else jnp.logical_not(low)
            q_aug = jnp.concatenate([jnp.where(own, q_pair, 0), hot], axis=1)
            s = nt(q_aug, k_aug)
            top = jnp.maximum(jnp.max(s, axis=1, keepdims=True), FLOOR)
            e = jnp.exp(s - top)
            total = jnp.maximum(jnp.sum(e, axis=1, keepdims=True), 0.5)
            outs.append(nn(e.astype(BF), v_pair) / total)
            stats = jnp.where(lane == 2 * pair + side, top + jnp.log(total), stats)
        ctx[rows, cols] = jnp.where(low, outs[0], outs[1]).astype(BF)
    return stats


def attn_fwd_kernel(
    tok, w_qkv, w_out, bias, hot, cold, qkv, ctx, lse, part, *, half, seq, blk
):
    qkv[...] = (nn(tok[...], w_qkv[...]) + bias[...]).astype(BF)

    def step(index, carry):
        rows = pl.ds(pl.multiple_of(index * blk, blk), blk)
        stats = attend(qkv, ctx, hot[0, rows, :], cold[0], rows, half)
        lse[0, :, rows] = stats.T[: lse.shape[1]]
        return carry

    lax.fori_loop(0, seq // blk, step, 0)
    part[...] = nn(ctx[...], w_out[...]).astype(BF)


def attn_fwd(tok, w_qkv, w_out, bias, hot, cold, rows, seq):
    width = tok.shape[1]
    half = width // 2
    stat_rows = -(-(half // HD) // 8) * 8
    whole = lambda shape: pl.BlockSpec(shape, lambda r: (0,) * len(shape))
    return pl.pallas_call(
        partial(attn_fwd_kernel, half=half, seq=seq, blk=256),
        grid=(rows,),
        in_specs=[
            pl.BlockSpec((seq, width), lambda r: (r, 0)),
            whole((width, 3 * half)),
            whole((half, width)),
            whole((1, 3 * half)),
            pl.BlockSpec((1, seq, LANES), lambda r: (r, 0, 0)),
            pl.BlockSpec((1, seq, LANES), lambda r: (r, 0, 0)),
        ],
        out_specs=[
            pl.BlockSpec((seq, 3 * half), lambda r: (r, 0)),
            pl.BlockSpec((seq, half), lambda r: (r, 0)),
            pl.BlockSpec((1, stat_rows, seq), lambda r: (r, 0, 0)),
            pl.BlockSpec((seq, width), lambda r: (r, 0)),
        ],
        out_shape=[
            jax.ShapeDtypeStruct((rows * seq, 3 * half), BF),
            jax.ShapeDtypeStruct((rows * seq, half), BF),
            jax.ShapeDtypeStruct((rows, stat_rows, seq), F32),
            jax.ShapeDtypeStruct((rows * seq, width), BF),
        ],
        compiler_params=params(),
        name="attn_fwd",
    )(tok, w_qkv, w_out, bias, hot, cold)


def attend_back(
    qkv, gctx, lse, centre, hot, cold, rows, half, gq_out, dk, dv, between=None
):
    blk = hot.shape[0]
    low = low_lanes((blk, LANES))
    scale = jnp.asarray(HD**-0.5, BF)
    sums = []
    for pair in range(half // LANES):
        if between is not None:
            between(pair)
        cols = pl.ds(pair * LANES, LANES)
        q_pair = qkv[rows, cols] * scale
        g_pair = gctx[rows, cols]
        k_pair = qkv[:, pl.ds(half + pair * LANES, LANES)]
        k_aug = jnp.concatenate([k_pair, cold], axis=1)
        v_pair = qkv[:, pl.ds(2 * half + pair * LANES, LANES)]
        outs = []
        dk_new = dk[:, cols]
        dv_new = dv[:, cols]
        for side in range(2):
            head = pl.ds(2 * pair + side, 1)
            own = low if side == 0 else jnp.logical_not(low)
            q_own = jnp.where(own, q_pair, 0)
            g_own = jnp.where(own, g_pair, 0)
            s = nt(k_aug, jnp.concatenate([q_own, hot], axis=1))
            p = jnp.exp(s - lse[head, rows])
            gp = nt(v_pair, g_own)
            gs = (p * (gp - centre[head, rows])).astype(BF)
            dv_new = dv_new + nn(p.astype(BF), g_own)
            dk_new = dk_new + nn(gs, q_own)
            outs.append(tn(gs, k_pair))
        dk[:, cols] = dk_new
        dv[:, cols] = dv_new
        gq = jnp.where(low, outs[0], outs[1]) * HD**-0.5
        gq_out[:, cols] = gq.astype(BF)
        sums.append(fold(gq))
    return jnp.concatenate(sums, axis=1)


def context_grad(gattn, ctx, w_out, gctx, centre, half):
    gctx[...] = nt(gattn[...], w_out[...]).astype(BF)
    prod = gctx[...].astype(F32) * ctx[...].astype(F32)
    picks = (
        lax.broadcasted_iota(jnp.int32, (8, half), 0)
        == lax.broadcasted_iota(jnp.int32, (8, half), 1) // HD
    ).astype(F32)
    centre[...] = lax.dot_general(
        picks, prod, (((1,), (1,)), ((), ())),
        preferred_element_type=F32, precision=lax.Precision.HIGHEST,
    )


def attn_bwd_kernel(
    gattn, qkv, ctx, lse, w_qkv, w_out, hot, cold, gqkv, sums, part, gctx, centre, dk, dv,
    *, half, seq, blk,
):
    context_grad(gattn, ctx, w_out, gctx, centre, half)
    dk[...] = jnp.zeros_like(dk)
    dv[...] = jnp.zeros_like(dv)

    def step(index, gq_sum):
        rows = pl.ds(pl.multiple_of(index * blk, blk), blk)
        out = gqkv.at[rows, pl.ds(0, half)]
        return gq_sum + attend_back(
            qkv, gctx, lse.at[0], centre, hot[0, rows, :], cold[0], rows, half, out, dk, dv
        )

    gq_sum = lax.fori_loop(0, seq // blk, step, jnp.zeros((1, half), F32))
    gqkv[:, pl.ds(half, half)] = dk[...].astype(BF)
    gqkv[:, pl.ds(2 * half, half)] = dv[...].astype(BF)
    sums[0, 0:1, :] = gq_sum
    sums[0, 1:2, :] = fold(dv[...])
    part[...] = nt(gqkv[...], w_qkv[...]).astype(BF)


def attn_bwd(gattn, qkv, ctx, lse, w_qkv, w_out, hot, cold, rows, seq):
    width = gattn.shape[1]
    half = width // 2
    whole = lambda shape: pl.BlockSpec(shape, lambda r: (0,) * len(shape))
    return pl.pallas_call(
        partial(attn_bwd_kernel, half=half, seq=seq, blk=256),
        grid=(rows,),
        in_specs=[
            pl.BlockSpec((seq, width), lambda r: (r, 0)),
            pl.BlockSpec((seq, 3 * half), lambda r: (r, 0)),
            pl.BlockSpec((seq, half), lambda r: (r, 0)),
            pl.BlockSpec((1, lse.shape[1], seq), lambda r: (r, 0, 0)),
            whole((width, 3 * half)),
            whole((half, width)),
            pl.BlockSpec((1, seq, LANES), lambda r: (r, 0, 0)),
            pl.BlockSpec((1, seq, LANES), lambda r: (r, 0, 0)),
        ],
        out_specs=[
            pl.BlockSpec((seq, 3 * half), lambda r: (r, 0)),
            pl.BlockSpec((1, 8, half), lambda r: (r, 0, 0)),
            pl.BlockSpec((seq, width), lambda r: (r, 0)),
        ],
        out_shape=[
            jax.ShapeDtypeStruct((rows * seq, 3 * half), BF),
            jax.ShapeDtypeStruct((rows, 8, half), F32),
            jax.ShapeDtypeStruct((rows * seq, width), BF),
        ],
        scratch_shapes=[
            pltpu.VMEM((seq, half), BF),
            pltpu.VMEM((8, seq), F32),
            pltpu.VMEM((seq, half), F32),
            pltpu.VMEM((seq, half), F32),
        ],
        compiler_params=params(),
        name="attn_bwd",
    )(gattn, qkv, ctx, lse, w_qkv, w_out, hot, cold)


def mean_last(x):
    return jnp.mean(x, axis=-1, keepdims=True)


def norm_back(grad, normal, inverse, gain):
    scaled = grad * gain
    return inverse * (scaled - mean_last(scaled) - normal * mean_last(scaled * normal))


def fold(x):
    return jnp.sum(x, axis=0, keepdims=True)


def feed_kernel(
    tok, cot, valid0, valid1, part, part_all, w_up, w_down, flat,
    out, r1_grad, gattn, grad_up, grad_down, sums, up_sum,
    got1, send, got2, got3, normal1, inv1, grad2, act, hid, gfeed, gpre, send_sem, recv_sem,
    *, tiles, blk,
):
    i = pl.program_id(0)
    me = lax.axis_index("tensor")
    other = 1 - me
    width = tok.shape[1]
    half = width // 2
    hidden = w_down.shape[0]
    chunk = width

    def span(t):
        return pl.ds(pl.multiple_of(t * blk, blk), blk)

    def copy(stage, t):
        return pltpu.make_async_remote_copy(
            src_ref=(part_all, send, send)[stage].at[span(t)],
            dst_ref=(got1, got2, got3)[stage].at[span(t)],
            send_sem=send_sem.at[stage, t],
            recv_sem=recv_sem.at[stage, t],
            device_id={"tensor": other},
            device_id_type=MESH,
        )

    @pl.when(i == 0)
    def _():
        barrier = pltpu.get_barrier_semaphore()
        pl.semaphore_signal(barrier, inc=1, device_id={"tensor": other}, device_id_type=MESH)
        pl.semaphore_wait(barrier, 1)
        for t in range(tiles):
            copy(0, t).start()
        sums[...] = jnp.zeros_like(sums)
        up_sum[...] = jnp.zeros_like(up_sum)

    def shared(piece):
        at = pl.ds(piece * half, half)
        return jnp.concatenate([flat[0:1, at], flat[1:2, at]], axis=1)

    bias_out, bias_down, gain1, shift1, gain2, shift2 = [shared(6 + n) for n in range(6)]
    b_up = flat[pl.ds(me, 1), pl.ds(2 * half, hidden)]

    @pl.when(i < tiles)
    def _():
        t = i
        slot = lax.rem(t, 3)
        copy(0, t).wait()
        keep = valid0[:, :1]
        att = part[...].astype(F32) + got1[span(t)].astype(F32) + bias_out
        r1 = tok[...].astype(F32) + att
        centred = r1 - mean_last(r1)
        inverse = lax.rsqrt(mean_last(centred * centred) + LN_EPS)
        normal = centred * inverse
        normal1[slot] = normal
        inv1[slot] = jnp.broadcast_to(inverse, (blk, LANES))
        low = (normal * gain1 + shift1).astype(BF)
        hid[span(t)] = low
        sums[6:7] += fold(keep * r1 * r1)
        sums[7:8] += fold(keep * att * att)
        for c in range(0, hidden, chunk):
            at = pl.ds(c, chunk)
            u = nn(low, w_up[c // chunk]) + b_up[:, c : c + chunk]
            both, gauss = erf_parts(u)
            act[span(t), at] = (0.5 * u * both).astype(BF)
            gpre[span(t), at] = (0.5 * both + u * gauss * INV_ROOT_TWO_PI).astype(BF)
        send[span(t)] = nn(act[span(t)], w_down[...]).astype(BF)
        copy(1, t).start()

    @pl.when((i >= 1) & (i <= tiles))
    def _():
        t = i - 1
        copy(1, t).wait()
        keep = valid1[:, :1]
        feed = send[span(t)].astype(F32) + got2[span(t)].astype(F32) + bias_down
        r2 = normal1[lax.rem(t, 3)] * gain1 + shift1 + feed
        centred = r2 - mean_last(r2)
        inverse = lax.rsqrt(mean_last(centred * centred) + LN_EPS)
        normal = centred * inverse
        out[...] = (normal * gain2 + shift2).astype(BF)
        g = cot[...].astype(F32) * keep
        gr = norm_back(g, normal, inverse, gain2)
        grad2[lax.rem(t, 2)] = gr
        sums[1:2] += fold(gr)
        sums[4:5] += fold(g * normal)
        sums[5:6] += fold(g)
        sums[8:9] += fold(keep * feed * feed)
        sums[9:10, :LANES] += fold(valid1[...])
        low = gr.astype(BF)
        gfeed[span(t)] = low
        total = jnp.zeros((blk, width), F32)
        for c in range(0, hidden, chunk):
            at = pl.ds(c, chunk)
            gu = nt(low, w_down[at]) * gpre[span(t), at].astype(F32)
            up_sum[0:1, at] += fold(gu)
            gu_low = gu.astype(BF)
            gpre[span(t), at] = gu_low
            total = total + nt(gu_low, w_up[c // chunk])
        send[span(t)] = total.astype(BF)
        copy(2, t).start()

    @pl.when(i == tiles + 1)
    def _():
        for c in range(0, hidden, half):
            grad_down[pl.ds(c, half)] = tn(act[:, c : c + half], gfeed[...]).astype(BF)

    @pl.when(i >= 2)
    def _():
        t = i - 2
        slot = lax.rem(t, 3)
        copy(2, t).wait()
        gh = grad2[lax.rem(t, 2)] + send[span(t)].astype(F32) + got3[span(t)].astype(F32)
        normal = normal1[slot]
        gr = norm_back(gh, normal, inv1[slot][:, :1], gain1)
        sums[0:1] += fold(gr)
        sums[2:3] += fold(gh * normal)
        sums[3:4] += fold(gh)
        r1_grad[...] = gr
        gattn[...] = gr.astype(BF)

    @pl.when(i == tiles + 1)
    def _():
        for c in range(0, hidden, chunk):
            for r in range(0, width, half):
                grad_up[c // chunk, pl.ds(r, half)] = tn(
                    hid[:, r : r + half], gpre[:, c : c + chunk]
                ).astype(BF)


def once(shape):
    return pl.BlockSpec(shape, lambda *i: (0,) * len(shape), pipeline_mode=pl.Buffered(1))


def feed(tok, cot, valid, part, w_up, w_down, flat, blk=256):
    count, width = tok.shape
    hidden = w_down.shape[0]
    tiles = count // blk
    lag = lambda n: (lambda i: (jnp.clip(i - n, 0, tiles - 1), 0))
    wide = lambda n: pl.BlockSpec((blk, width), lag(n))
    return pl.pallas_call(
        partial(feed_kernel, tiles=tiles, blk=blk),
        grid=(tiles + 2,),
        in_specs=[
            wide(0),
            wide(1),
            pl.BlockSpec((blk, LANES), lag(0)),
            pl.BlockSpec((blk, LANES), lag(1)),
            wide(0),
            pl.BlockSpec(memory_space=pl.ANY),
            once(w_up.shape),
            once((hidden, width)),
            once(flat.shape),
        ],
        out_specs=[
            wide(1), wide(2), wide(2), once(w_up.shape), once((hidden, width)),
            once((16, width)), once((8, hidden)),
        ],
        out_shape=[
            jax.ShapeDtypeStruct((count, width), BF),
            jax.ShapeDtypeStruct((count, width), F32),
            jax.ShapeDtypeStruct((count, width), BF),
            jax.ShapeDtypeStruct(w_up.shape, BF),
            jax.ShapeDtypeStruct((hidden, width), BF),
            jax.ShapeDtypeStruct((16, width), F32),
            jax.ShapeDtypeStruct((8, hidden), F32),
        ],
        scratch_shapes=[
            *[pltpu.VMEM((count, width), BF) for _ in range(4)],
            pltpu.VMEM((3, blk, width), F32),
            pltpu.VMEM((3, blk, LANES), F32),
            pltpu.VMEM((2, blk, width), F32),
            pltpu.VMEM((count, hidden), BF),
            pltpu.VMEM((count, width), BF),
            pltpu.VMEM((count, width), BF),
            pltpu.VMEM((count, hidden), BF),
            pltpu.SemaphoreType.DMA((3, tiles)),
            pltpu.SemaphoreType.DMA((3, tiles)),
        ],
        compiler_params=params(collective_id=1, has_side_effects=True),
        name="feed",
    )(tok, cot, valid, valid, part, part, w_up, w_down, flat)


PLANE = 4
DEPTH = 4
UP, DOWN, ALONG_X, ALONG_Y = 0, 1, 2, 3


def where_am_i():
    dp = lax.axis_index("dp")
    return dp, dp // PLANE, lax.rem(dp, PLANE)


def flip(xy, bit):
    step = 1 if bit == ALONG_X else 2
    side = lax.rem(xy // step, 2)
    return xy + step - 2 * step * side


def toward(direction):
    dp, z, xy = where_am_i()
    if direction == UP:
        return dp + PLANE
    if direction == DOWN:
        return dp - PLANE
    return z * PLANE + flip(xy, direction)


def greet():
    dp, z, xy = where_am_i()
    barrier = pltpu.get_barrier_semaphore()
    other = 1 - lax.axis_index("tensor")

    def tell(device):
        pl.semaphore_signal(barrier, inc=1, device_id=device, device_id_type=MESH)

    tell({"tensor": other})
    tell({"dp": toward(ALONG_X)})
    tell({"dp": toward(ALONG_Y)})
    pl.when(z < DEPTH - 1)(lambda: tell({"dp": toward(UP)}))
    pl.when(z > 0)(lambda: tell({"dp": toward(DOWN)}))
    inner = jnp.logical_and(z < DEPTH - 1, z > 0)
    pl.semaphore_wait(barrier, jnp.where(inner, 5, 4))


class Gather:
    def __init__(self, kinds, send_sem, recv_sem):
        self.kinds = kinds
        self.send_sem, self.recv_sem = send_sem, recv_sem
        self.dp, self.z, self.xy = where_am_i()

    def copy(self, c, direction, origin, part):
        place, first, rows = self.kinds[c]
        ref = place(origin)
        if part == 1:
            ref = ref.at[pl.ds(0, first)]
        if part == 2:
            ref = ref.at[pl.ds(first, rows - first)]
        slot = origin if part != 2 else DEPTH * PLANE + origin // PLANE
        lane = direction if part == 0 else direction + 2
        return pltpu.make_async_remote_copy(
            src_ref=ref,
            dst_ref=ref,
            send_sem=self.send_sem.at[c, lane, origin],
            recv_sem=self.recv_sem.at[c, slot],
            device_id={"dp": toward(direction)},
            device_id_type=MESH,
        )

    def send(self, ok, c, direction, origin, part=0):
        start = lambda: self.copy(c, direction, origin, part).start()
        start() if ok is None else pl.when(ok)(start)

    def levels(self, k):
        if k == 0:
            return [(None, self.z)]
        below, above = self.z - k, self.z + k
        return [(below >= 0, below), (above < DEPTH, above)]

    def along(self, c, k):
        for ok, level in self.levels(k):
            origin = level * PLANE + self.xy
            up, down = self.z < DEPTH - 1, self.z > 0
            if k == 0:
                self.send(up, c, UP, origin)
                self.send(down, c, DOWN, origin)
            else:
                pl.when(ok)(lambda: self.copy(c, ALONG_X, origin, 0).wait_recv())
                from_below = level < self.z
                self.send(ok & from_below & up, c, UP, origin)
                self.send(ok & jnp.logical_not(from_below) & down, c, DOWN, origin)
            self.send(ok, c, ALONG_X, origin)
            self.send(ok, c, ALONG_Y, origin)

    def across(self, c, k):
        first, rows = self.kinds[c][1:]
        for ok, level in self.levels(k):
            for came, onward, part in ((ALONG_X, ALONG_Y, 1), (ALONG_Y, ALONG_X, 2)):
                origin = level * PLANE + flip(self.xy, came)
                wait = lambda came=came, origin=origin: self.copy(c, came, origin, 0).wait_recv()
                wait() if ok is None else pl.when(ok)(wait)
                if part == 1 or rows > first:
                    self.send(ok, c, onward, origin, part if rows > first else 3)

    def last(self, c):
        first, rows = self.kinds[c][1:]
        diag = flip(flip(self.xy, ALONG_X), ALONG_Y)
        for level in range(DEPTH):
            origin = level * PLANE + diag
            if rows > first:
                self.copy(c, ALONG_Y, origin, 1).wait_recv()
                self.copy(c, ALONG_X, origin, 2).wait_recv()
            else:
                self.copy(c, ALONG_Y, origin, 3).wait_recv()

    def sent(self):
        for c, (_, first, rows) in enumerate(self.kinds):
            left = lambda *what: self.copy(c, *what).wait_send()
            for level in range(DEPTH):
                here = level * PLANE + self.xy
                up = jnp.logical_and(level <= self.z, self.z < DEPTH - 1)
                down = jnp.logical_and(level >= self.z, self.z > 0)
                pl.when(up)(lambda: left(UP, here, 0))
                pl.when(down)(lambda: left(DOWN, here, 0))
                left(ALONG_X, here, 0)
                left(ALONG_Y, here, 0)
                beside = level * PLANE + flip(self.xy, ALONG_X)
                left(ALONG_Y, beside, 1 if rows > first else 3)
                if rows > first:
                    left(ALONG_X, level * PLANE + flip(self.xy, ALONG_Y), 2)


class Scatter:
    def __init__(self, kinds, send_sem, recv_sem):
        self.kinds = kinds
        self.send_sem, self.recv_sem = send_sem, recv_sem
        self.dp, self.z, self.xy = where_am_i()

    def term(self, c, column, level):
        return self.kinds[c][0](level * PLANE + column)

    def copy(self, c, what, level, direction=None):
        first, rows, _, got = self.kinds[c][1:]
        column, way = (
            (flip(flip(self.xy, ALONG_X), ALONG_Y), ALONG_Y),
            (flip(flip(self.xy, ALONG_X), ALONG_Y), ALONG_X),
            (flip(self.xy, ALONG_X), ALONG_X),
            (flip(self.xy, ALONG_Y), ALONG_Y),
            (self.xy, UP),
            (self.xy, DOWN),
        )[what]
        src = self.term(c, column, level)
        if what == 0:
            src = src.at[pl.ds(0, first)]
        if what == 1:
            src = src.at[pl.ds(first, rows - first)]
        return pltpu.make_async_remote_copy(
            src_ref=src,
            dst_ref=got[what].at[level],
            send_sem=self.send_sem.at[c, what, level],
            recv_sem=self.recv_sem.at[c, what, level],
            device_id={"dp": toward(way if direction is None else direction)},
            device_id_type=MESH,
        )

    def start(self, c, what, level):
        self.copy(c, what, level).start()

    def came(self, c, what, level):
        self.copy(c, what, level, ALONG_X).wait_recv()

    def left(self, c, what, level):
        self.copy(c, what, level, ALONG_X).wait_send()

    def split(self, c):
        return self.kinds[c][2] > self.kinds[c][1]

    def first(self, c, level):
        self.start(c, 0, level)
        if self.split(c):
            self.start(c, 1, level)

    def second(self, c, level):
        first, rows, _, got = self.kinds[c][1:]
        a, b = pl.ds(0, first), pl.ds(first, rows - first)
        own_x = self.term(c, flip(self.xy, ALONG_X), level)
        own_y = self.term(c, flip(self.xy, ALONG_Y), level)
        add = lambda p, q: (p.astype(F32) + q.astype(F32)).astype(p.dtype)
        self.came(c, 0, level)
        own_x[a] = add(own_x[a], got[0][level])
        self.start(c, 2, level)
        if self.split(c):
            self.came(c, 1, level)
            own_y[b] = add(own_y[b], got[1][level])
        self.start(c, 3, level)

    def third(self, c, level):
        total, got = self.kinds[c][3:]
        own = self.term(c, self.xy, level)
        self.came(c, 2, level)
        self.came(c, 3, level)
        here = own[...].astype(F32) + got[2][level].astype(F32) + got[3][level].astype(F32)

        @pl.when(level == self.z)
        def _():
            total[...] = here

        for what, beyond, more in (
            (4, level > self.z, self.z > 0),
            (5, level < self.z, self.z < DEPTH - 1),
        ):

            @pl.when(jnp.logical_and(beyond, jnp.logical_not(more)))
            def _():
                own[...] = here.astype(own.dtype)
                self.start(c, what, level)

            @pl.when(jnp.logical_and(beyond, more))
            def _():
                self.came(c, what, level)
                own[...] = (here + got[what][level].astype(F32)).astype(own.dtype)
                self.start(c, what, level)

    def last(self, c):
        total, got = self.kinds[c][3:]
        for what, more in ((4, self.z > 0), (5, self.z < DEPTH - 1)):

            @pl.when(more)
            def _():
                self.came(c, what, self.z)
                total[...] += got[what][self.z].astype(F32)

    def sent(self, c):
        for level in range(DEPTH):
            self.left(c, 0, level)
            if self.split(c):
                self.left(c, 1, level)
            self.left(c, 2, level)
            self.left(c, 3, level)
            pl.when(level > self.z)(lambda: self.left(c, 4, level))
            pl.when(level < self.z)(lambda: self.left(c, 5, level))


def landing(first, rows, cols, kind):
    halves = [(DEPTH, first, cols), (DEPTH, max(rows - first, first), cols)]
    return [pltpu.VMEM(shape, kind) for shape in halves + [(DEPTH, rows, cols)] * 4]


GATHER_SLOTS = DEPTH * PLANE + DEPTH
KINDS = 3
VEC_ROWS = 8


def step_at(position, pair):
    i, j = divmod(position, 3)
    return pl.program_id(0) == i if pair == j else None


def play(schedule, pair):
    for position, work in schedule:
        now = step_at(position, pair)
        if now is not None:

            @pl.when(now)
            def _():
                work()


def front_kernel(
    tok, hot, cold, mat, vec,
    qkv, ctx, lse, part, flat, wk_out, w_out, w1_out, w2_out,
    wk, w1, w2, vecs, wo, send_sem, recv_sem, swap_sem, out_sem,
    *, edge, per, seq, blk, steps,
):
    i = pl.program_id(0)
    width = tok.shape[1]
    half = width // 2
    shard = vec.shape[1]
    own = lax.axis_index("tensor")

    def place0(d):
        rows = pl.ds(pl.multiple_of(lax.rem(d, PLANE) * 2 * edge, 2 * edge), 2 * edge)
        return wk.at[rows, pl.ds(pl.multiple_of(d // PLANE * half, half), half)]

    def place1(d):
        return w1.at[lax.rem(d, 2), pl.ds(pl.multiple_of(d // 2 * edge, edge), edge)]

    def place2(d):
        return w2.at[pl.ds(pl.multiple_of(d * edge, edge), edge)]

    def place3(d):
        return vecs.at[own, d]

    gather = Gather(
        [
            (place3, VEC_ROWS, VEC_ROWS),
            (place0, edge, 2 * edge),
            (place1, edge // 2, edge),
            (place2, edge // 2, edge),
        ],
        send_sem,
        recv_sem,
    )
    swap = pltpu.make_async_remote_copy(
        src_ref=vecs.at[own],
        dst_ref=vecs.at[own],
        send_sem=swap_sem.at[0],
        recv_sem=swap_sem.at[1],
        device_id={"tensor": 1 - own},
        device_id_type=MESH,
    )
    saves = [
        pltpu.make_async_copy(src, dst, out_sem.at[n])
        for n, (src, dst) in enumerate(((wk, wk_out), (wo, w_out), (w1, w1_out), (w2, w2_out)))
    ]
    dp = gather.dp

    @pl.when(i == 0)
    def _():
        mine0, mine1, mine2 = place0(dp), place1(dp), place2(dp)
        for j in range(per):
            at = pl.ds(j % (per // 2) * edge, edge)
            mine0[pl.ds(j // (per // 2) * edge, edge), at] = mat[j].astype(BF)
        place3(dp)[...] = jnp.zeros(vecs.shape[2:], F32)
        place3(dp)[0:1, pl.ds(0, shard)] = vec[...]
        greet()
        gather.along(1, 0)
        gather.along(0, 0)
        for j in range(per):
            mine1[:, pl.ds(j * edge, edge)] = mat[per + j].astype(BF)
            mine2[:, pl.ds(j * edge, edge)] = mat[2 * per + j].astype(BF)
        for k in range(1, DEPTH):
            gather.along(1, k)
            gather.along(0, k)
            gather.across(1, k - 1)
            gather.across(0, k - 1)
        gather.across(1, DEPTH - 1)
        gather.across(0, DEPTH - 1)
        gather.along(2, 0)
        gather.last(0)
        swap.start()
        gather.last(1)
        gather.along(3, 0)
        saves[0].start()
        for j in range(width // edge):
            wo[pl.ds(j // 2 * edge, edge), pl.ds(j % 2 * half, half)] = wk[
                pl.ds(j * edge, edge), pl.ds(3 * half, half)
            ]
        saves[1].start()
        swap.wait()
        flat[...] = jnp.zeros_like(flat)
        for t in range(2):
            for d in range(DEPTH * PLANE):
                flat[t : t + 1, pl.ds(d * shard, shard)] = vecs[t, d, 0:1, pl.ds(0, shard)]

    @pl.when(lax.rem(i, steps) == 0)
    def _():
        bq, bv = flat[pl.ds(own, 1), pl.ds(0, half)], flat[pl.ds(own, 1), pl.ds(half, half)]
        bias = jnp.concatenate([bq, jnp.zeros_like(bq), bv], axis=1)
        qkv[...] = (nn(tok[...], wk[:, pl.ds(0, 3 * half)]) + bias).astype(BF)

    schedule = [
        (3, lambda: (gather.along(2, 1), gather.across(2, 0))),
        (5, lambda: (gather.along(3, 1), gather.across(3, 0))),
        (7, lambda: (gather.along(2, 2), gather.across(2, 1))),
        (9, lambda: (gather.along(3, 2), gather.across(3, 1))),
        (11, lambda: (gather.along(2, 3), gather.across(2, 2))),
        (13, lambda: (gather.along(3, 3), gather.across(3, 2))),
        (16, lambda: gather.across(2, 3)),
        (18, lambda: gather.across(3, 3)),
        (20, lambda: (gather.last(2), saves[2].start())),
    ]
    rows = pl.ds(pl.multiple_of(lax.rem(i, steps) * blk, blk), blk)
    stats = attend(
        qkv, ctx, hot[0, rows, :], cold[0], rows, half, lambda pair: play(schedule, pair)
    )
    lse[0, :, rows] = stats.T[: lse.shape[1]]

    @pl.when(lax.rem(i, steps) == steps - 1)
    def _():
        part[...] = nn(ctx[...], wo[...]).astype(BF)

    @pl.when(i == pl.num_programs(0) - 1)
    def _():
        gather.last(3)
        saves[3].start()
        gather.sent()
        for save in saves:
            save.wait()


def front(tok, hot, cold, mat, vec, rows, seq, blk=256):
    per, edge = mat.shape[0] // KINDS, mat.shape[-1]
    count, width = tok.shape
    half = width // 2
    stat_rows = -(-(half // HD) // 8) * 8
    chips = DEPTH * PLANE
    steps = seq // blk
    row = lambda shape: pl.BlockSpec(shape, lambda i: (i // steps,) + (0,) * (len(shape) - 1))
    hbm = pl.BlockSpec(memory_space=pl.ANY)
    weights = [(width, 2 * width), (half, width), (2, width, width), (2 * width, width)]
    return pl.pallas_call(
        partial(front_kernel, edge=edge, per=per, seq=seq, blk=blk, steps=steps),
        grid=(rows * steps,),
        in_specs=[
            row((seq, width)),
            row((1, seq, LANES)),
            row((1, seq, LANES)),
            once(mat.shape),
            once(vec.shape),
        ],
        out_specs=[
            row((seq, 3 * half)),
            row((seq, half)),
            row((1, stat_rows, seq)),
            row((seq, width)),
            once((8, chips * vec.shape[1])),
            *[hbm] * 4,
        ],
        out_shape=[
            jax.ShapeDtypeStruct((count, 3 * half), BF),
            jax.ShapeDtypeStruct((count, half), BF),
            jax.ShapeDtypeStruct((rows, stat_rows, seq), F32),
            jax.ShapeDtypeStruct((count, width), BF),
            jax.ShapeDtypeStruct((8, chips * vec.shape[1]), F32),
            *[jax.ShapeDtypeStruct(shape, BF) for shape in weights],
        ],
        scratch_shapes=[
            pltpu.VMEM(weights[0], BF),
            pltpu.VMEM(weights[2], BF),
            pltpu.VMEM(weights[3], BF),
            pltpu.VMEM((2, chips, VEC_ROWS, -(-vec.shape[1] // LANES) * LANES), F32),
            pltpu.VMEM(weights[1], BF),
            pltpu.SemaphoreType.DMA((4, 6, chips)),
            pltpu.SemaphoreType.DMA((4, GATHER_SLOTS)),
            pltpu.SemaphoreType.DMA((2,)),
            pltpu.SemaphoreType.DMA((4,)),
        ],
        compiler_params=params(collective_id=2, has_side_effects=True),
        name="front",
    )(tok, hot, cold, mat, vec)


def back_kernel(
    gattn, qkv, ctx, lse, wk, w_out, hot, cold, sums, up_sum, r1_grad, tok_all, g1_in, g2_in,
    input_grad, tot0, tot1, tot2, totv,
    tok, g0, g1, g2, gv, gqkv, gctx, centre, dk, dv, out_grad, bias_sums, part, got_part,
    *rest, edge, per, steps, row_count, blk, shard,
):
    i = pl.program_id(0)
    count, width = tok.shape
    half = width // 2
    seq = gctx.shape[0]
    compute = row_count * steps
    me = lax.axis_index("tensor")
    gots, (send_sem, recv_sem, part_sem, load_sem) = rest[:-4], rest[-4:]
    gots = [gots[c * 6 : (c + 1) * 6] for c in range(4)]

    def place0(d):
        return g0.at[d]

    def place1(d):
        return g1.at[lax.rem(d, 2), pl.ds(pl.multiple_of(d // 2 * edge, edge), edge)]

    def place2(d):
        return g2.at[pl.ds(pl.multiple_of(d * edge, edge), edge)]

    def place3(d):
        return gv.at[d]

    VEC, DOWN_W, UP_W, ATT = range(4)
    scatter = Scatter(
        [
            (place3, VEC_ROWS, VEC_ROWS, totv, gots[VEC]),
            (place2, edge // 2, edge, tot2, gots[DOWN_W]),
            (place1, edge // 2, edge, tot1, gots[UP_W]),
            (place0, edge, 2 * edge, tot0, gots[ATT]),
        ],
        send_sem,
        recv_sem,
    )
    far_first = [jnp.where(scatter.z < DEPTH // 2, DEPTH - 1 - k, k) for k in range(DEPTH)]
    loads = [
        pltpu.make_async_copy(src, dst, load_sem.at[n])
        for n, (src, dst) in enumerate(((g2_in, g2), (g1_in, g1), (tok_all, tok)))
    ]

    def swap(r):
        at = pl.ds(pl.multiple_of(r * seq, seq), seq)
        return pltpu.make_async_remote_copy(
            src_ref=part.at[at],
            dst_ref=got_part.at[at],
            send_sem=part_sem.at[0, r],
            recv_sem=part_sem.at[1, r],
            device_id={"tensor": 1 - me},
            device_id_type=MESH,
        )

    @pl.when(i == 0)
    def _():
        for load in loads:
            load.start()
        greet()

    def begin(c, load):
        loads[load].wait()
        for k in range(DEPTH):
            scatter.first(c, far_first[k])

    second = lambda c, k: (lambda: scatter.second(c, far_first[k]))
    third = lambda c, k: (lambda: scatter.third(c, far_first[k]))
    schedule = [
        (0, lambda: begin(DOWN_W, 0)),
        (1, lambda: begin(UP_W, 1)),
        (2, second(DOWN_W, 0)),
        (3, second(DOWN_W, 1)),
        (4, second(DOWN_W, 2)),
        (5, second(DOWN_W, 3)),
        (6, lambda: (third(DOWN_W, 0)(), second(UP_W, 0)())),
        (7, lambda: (third(DOWN_W, 1)(), second(UP_W, 1)())),
        (8, lambda: (third(DOWN_W, 2)(), second(UP_W, 2)())),
        (9, lambda: (third(DOWN_W, 3)(), second(UP_W, 3)())),
        (12, third(UP_W, 0)),
        (13, lambda: (third(UP_W, 1)(), scatter.first(ATT, 3))),
        (14, third(UP_W, 2)),
        (15, third(UP_W, 3)),
        (17, lambda: (scatter.last(DOWN_W), scatter.second(ATT, 3))),
        (19, lambda: scatter.last(UP_W)),
        (21, lambda: scatter.third(ATT, 3)),
    ]

    @pl.when((lax.rem(i, steps) == 0) & (i < compute))
    def _():
        context_grad(gattn, ctx, w_out, gctx, centre, half)
        dk[...] = jnp.zeros_like(dk)
        dv[...] = jnp.zeros_like(dv)

        @pl.when(i == 0)
        def _():
            out_grad[...] = jnp.zeros_like(out_grad)
            bias_sums[...] = jnp.zeros_like(bias_sums)

        out_grad[...] += tn(ctx[...], gattn[...])

        @pl.when(i == compute - steps)
        def _():
            for j in range(2 * PLANE):
                g0[3 * PLANE + j // 2, pl.ds(j % 2 * edge, edge)] = out_grad[
                    pl.ds(j // 2 * edge, edge), pl.ds(j % 2 * half, half)
                ].astype(BF)

    @pl.when(i < compute)
    def _():
        row = i // steps
        at = pl.multiple_of(lax.rem(i, steps) * blk, blk)
        rows = pl.ds(at, blk)
        there = pl.ds(pl.multiple_of(row * seq + at, blk), blk)
        bias_sums[0:1] += attend_back(
            qkv, gctx, lse.at[0], centre, hot[0, rows, :], cold[0], rows, half,
            gqkv.at[there, pl.ds(0, half)], dk, dv, lambda pair: play(schedule, pair),
        )

        @pl.when(lax.rem(i, steps) == steps - 1)
        def _():
            whole = pl.ds(pl.multiple_of(row * seq, seq), seq)
            gqkv[whole, pl.ds(half, half)] = dk[...].astype(BF)
            gqkv[whole, pl.ds(2 * half, half)] = dv[...].astype(BF)
            bias_sums[1:2] += fold(dv[...])
            part[whole] = nt(gqkv[whole], wk[:, pl.ds(0, 3 * half)]).astype(BF)
            swap(row).start()

    @pl.when(i == compute - 1)
    def _():
        loads[2].wait()
        flat = [bias_sums[0:1], bias_sums[1:2], up_sum[0:1]]
        flat += [sums[0:6, pl.ds(pl.multiple_of(me * half, half), half)][n : n + 1] for n in range(6)]
        flat = jnp.concatenate(flat, axis=1)
        sizes = sums[6:10, 0:LANES]
        for n in range(1, width // LANES):
            sizes = sizes + sums[6:10, pl.ds(n * LANES, LANES)]
        gv[...] = jnp.zeros_like(gv)
        for d in range(DEPTH * PLANE):
            gv[d, 0:1, pl.ds(0, shard)] = flat[:, d * shard : (d + 1) * shard]
            gv[d, 1:5, pl.ds(0, LANES)] = sizes
        for n in (2, 1, 0):
            grad = tn(tok[...], gqkv[:, pl.ds(n * half, half)]).astype(BF)
            for j in range(PLANE):
                g0[n * PLANE + j] = grad[2 * edge * j : 2 * edge * (j + 1)]
            scatter.first(ATT, n)
            if n == 2:
                for k in range(DEPTH):
                    scatter.first(VEC, k)
        for n in (2, 1, 0):
            scatter.second(ATT, n)
        for k in range(DEPTH):
            scatter.second(VEC, k)

    @pl.when(i >= steps)
    def _():
        chunk = i - steps
        row = chunk // steps
        pl.when(lax.rem(chunk, steps) == 0)(lambda: swap(row).wait())
        at = pl.ds(pl.multiple_of(chunk * blk, blk), blk)
        input_grad[...] = r1_grad[...] + part[at].astype(F32) + got_part[at].astype(F32)

    @pl.when(i == compute + steps - 1)
    def _():
        for n in (2, 1, 0):
            scatter.third(ATT, n)
        for k in range(DEPTH):
            scatter.third(VEC, k)
        scatter.last(ATT)
        scatter.last(VEC)
        for c in range(4):
            scatter.sent(c)


def back(gattn, qkv, ctx, lse, wk, w_out, hot, cold, sums, up_sum, r1_grad, tok, g1, g2, rows, seq, shard, blk=256):
    count, width = tok.shape
    half = width // 2
    edge = width // 8
    chips = DEPTH * PLANE
    steps = seq // blk
    compute = rows * steps
    row = lambda shape: pl.BlockSpec(
        shape, lambda i: (jnp.minimum(i // steps, rows - 1),) + (0,) * (len(shape) - 1)
    )
    late = pl.BlockSpec((blk, width), lambda i: (jnp.maximum(i - steps, 0), 0))
    hbm = pl.BlockSpec(memory_space=pl.ANY)
    wide = -(-shard // LANES) * LANES
    return pl.pallas_call(
        partial(back_kernel, edge=edge, per=8, steps=steps, row_count=rows, blk=blk, shard=shard),
        grid=(compute + steps,),
        in_specs=[
            row((seq, width)),
            row((seq, 3 * half)),
            row((seq, half)),
            row((1, lse.shape[1], seq)),
            once(wk.shape),
            once(w_out.shape),
            row((1, seq, LANES)),
            row((1, seq, LANES)),
            once(sums.shape),
            once(up_sum.shape),
            late,
            hbm,
            hbm,
            hbm,
        ],
        out_specs=[
            late,
            once((2 * edge, half)),
            once((edge, width)),
            once((edge, width)),
            once((VEC_ROWS, wide)),
        ],
        out_shape=[
            jax.ShapeDtypeStruct((count, width), F32),
            jax.ShapeDtypeStruct((2 * edge, half), F32),
            jax.ShapeDtypeStruct((edge, width), F32),
            jax.ShapeDtypeStruct((edge, width), F32),
            jax.ShapeDtypeStruct((VEC_ROWS, wide), F32),
        ],
        scratch_shapes=[
            pltpu.VMEM((count, width), BF),
            pltpu.VMEM((chips, 2 * edge, half), BF),
            pltpu.VMEM(g1.shape, BF),
            pltpu.VMEM(g2.shape, BF),
            pltpu.VMEM((chips, VEC_ROWS, wide), F32),
            pltpu.VMEM((count, 3 * half), BF),
            pltpu.VMEM((seq, half), BF),
            pltpu.VMEM((8, seq), F32),
            pltpu.VMEM((seq, half), F32),
            pltpu.VMEM((seq, half), F32),
            pltpu.VMEM((half, width), F32),
            pltpu.VMEM((8, half), F32),
            pltpu.VMEM((count, width), BF),
            pltpu.VMEM((count, width), BF),
            *landing(VEC_ROWS, VEC_ROWS, wide, F32),
            *landing(edge // 2, edge, width, BF),
            *landing(edge // 2, edge, width, BF),
            *landing(edge, 2 * edge, half, BF),
            pltpu.SemaphoreType.DMA((4, 6, DEPTH)),
            pltpu.SemaphoreType.DMA((4, 6, DEPTH)),
            pltpu.SemaphoreType.DMA((2, rows)),
            pltpu.SemaphoreType.DMA((3,)),
        ],
        compiler_params=params(collective_id=3, has_side_effects=True),
        name="back",
    )(gattn, qkv, ctx, lse, wk, w_out, hot, cold, sums, up_sum, r1_grad, tok, g1, g2)


def step_kernel(t0, t1, t2, master, left, right, root_l, root_r, grads, left_new, right_new, mat_new):
    kind = pl.program_id(0)
    per, edge = master.shape[0], master.shape[-1]

    def block(j, grad):
        low = grad.astype(BF)
        grads[j] = grad
        left_new[j] = DECAY * left[j] + (1.0 - DECAY) * nt(low, low)
        right_new[j] = DECAY * right[j] + (1.0 - DECAY) * tn(low, low)
        turned = nn(root_l[j].astype(BF), low).astype(BF)
        mat_new[j] = master[j] - STEP_RATE * nn(turned, root_r[j].astype(BF))

    @pl.when(kind == 0)
    def _():
        half = per // 2
        for j in range(per):
            block(j, t0[pl.ds(j // half * edge, edge), pl.ds(j % half * edge, edge)])

    for number, total in ((1, t1), (2, t2)):

        @pl.when(kind == number)
        def _():
            for j in range(per):
                block(j, total[:, pl.ds(j * edge, edge)])


def take_step(t0, t1, t2, master, left, right, root_l, root_r):
    per, edge = master.shape[0] // KINDS, master.shape[-1]
    blocks = pl.BlockSpec((per, edge, edge), lambda k: (k, 0, 0))
    return pl.pallas_call(
        step_kernel,
        grid=(KINDS,),
        in_specs=[once(t0.shape), once(t1.shape), once(t2.shape), *[blocks] * 5],
        out_specs=[blocks] * 4,
        out_shape=[jax.ShapeDtypeStruct(master.shape, F32)] * 4,
        compiler_params=params(),
        name="take_step",
    )(t0, t1, t2, master, left, right, root_l, root_r)


def far_weights(mat_master, vec_master, width):
    half = width // 2
    edge = mat_master.shape[-1]
    local = mat_master.astype(BF).reshape(KINDS, -1, edge, edge)
    blocks = lax.all_gather(local, "dp", axis=1, tiled=True)
    kind_count = blocks.shape[1]
    quarter = kind_count // 4
    grid_model = width // edge
    grid_half = half // edge
    grid_hidden = kind_count // grid_model
    w_project = (
        blocks[0, : 3 * quarter]
        .reshape(3, grid_model, grid_half, edge, edge)
        .transpose(1, 3, 0, 2, 4)
        .reshape(width, 3 * half)
    )
    w_out = unblock(blocks[0, 3 * quarter :], grid_half, grid_model)
    w_up = unblock(blocks[1], grid_model, grid_hidden).reshape(width, -1, width)
    w_down = unblock(blocks[2], grid_hidden, grid_model)
    shard = vec_master.shape[0]
    every = lax.all_gather(vec_master, ("dp", "tensor"), axis=0, tiled=True)
    flat = every.reshape(-1, 2, shard).transpose(1, 0, 2).reshape(2, 12 * half)
    return w_project, w_out, w_up.transpose(1, 0, 2), w_down, jnp.pad(flat, ((0, 6), (0, 0)))


def far_step(grads, state):
    grad_project, grad_out_weight, grad_up, grad_down, vec_local, sizes = grads
    mat_master, mat_left, mat_right, root_left, root_right = state
    edge = mat_master.shape[-1]
    width, half = grad_project.shape[0], grad_project.shape[1] // 3
    project_blocks = (
        grad_project.reshape(width // edge, edge, 3, half // edge, edge)
        .transpose(2, 0, 3, 1, 4)
        .reshape(-1, edge, edge)
    )
    attention_blocks = jnp.concatenate([project_blocks, to_blocks(grad_out_weight, edge)], axis=0)
    grad_up = grad_up.transpose(1, 0, 2).reshape(width, -1)
    owned = lax.psum_scatter(
        jnp.stack([attention_blocks, to_blocks(grad_up, edge), to_blocks(grad_down, edge)]),
        "dp",
        scatter_dimension=1,
        tiled=True,
    )
    vec_grads = lax.psum_scatter(vec_local, "dp", scatter_dimension=0, tiled=True)
    mat_grads = owned.astype(F32).reshape(-1, edge, edge)
    left_new = DECAY * mat_left + (1.0 - DECAY) * jnp.einsum("bij,bkj->bik", mat_grads, mat_grads)
    right_new = DECAY * mat_right + (1.0 - DECAY) * jnp.einsum("bji,bjk->bik", mat_grads, mat_grads)
    turned = jnp.einsum("bij,bjk->bik", root_left, mat_grads)
    turned = jnp.einsum("bij,bjk->bik", turned, root_right)
    mat_new = mat_master - STEP_RATE * turned
    return (mat_grads, left_new, right_new, mat_new), vec_grads, lax.psum(sizes, "dp")


def body(
    tokens,
    cotangent,
    pair_lengths,
    mat_master,
    mat_left,
    mat_right,
    root_left,
    root_right,
    vec_master,
    vec_second,
):
    width = tokens.shape[1]
    half = width // 2
    row_count, pair_count = pair_lengths.shape
    seq = tokens.shape[0] // row_count
    edge = mat_master.shape[-1]
    shard = vec_master.shape[0]
    own_index = lax.axis_index("tensor")
    near = lax.axis_size("dp") == DEPTH * PLANE and mat_master.shape[0] == KINDS * width // edge

    place = lax.broadcasted_iota(jnp.int32, (row_count, seq, pair_count), 1)
    upto = jnp.tril(jnp.ones((pair_count, pair_count), jnp.int32))
    ends = jnp.sum(pair_lengths[:, None, :] * upto[None], axis=-1)
    pairs = jnp.sum((place >= ends[:, None, :]).astype(jnp.int32), axis=-1)
    ids = lax.broadcasted_iota(jnp.int32, (row_count, seq, LANES), 2)
    same = pairs[:, :, None] == ids
    hot = same.astype(BF)
    cold = jnp.where(same & (ids < pair_count), 0.0, -BIG).astype(BF)
    keep = (pairs < pair_count).astype(F32).reshape(-1)
    valid = jnp.broadcast_to(keep[:, None], (keep.shape[0], LANES))
    state = (mat_master, mat_left, mat_right, root_left, root_right)

    if near:
        qkv, ctx, lse, part, flat, wk, w_out, w_up, w_down = front(
            tokens, hot, cold, mat_master, vec_master[None], row_count, seq
        )
    else:
        w_project, w_out, w_up, w_down, flat = far_weights(mat_master, vec_master, width)
        own = lax.dynamic_slice_in_dim(flat, own_index, 1)
        bias = jnp.concatenate([own[:, :half], jnp.zeros((1, half), F32), own[:, half : 2 * half]], axis=1)
        qkv, ctx, lse, part = attn_fwd(tokens, w_project, w_out, bias, hot, cold, row_count, seq)
    block_out, gr1, gattn, grad_up, grad_down, sums, up_sum = feed(
        tokens, cotangent, valid, part, w_up, w_down, flat
    )
    if near:
        input_grad, tot0, tot1, tot2, totv = back(
            gattn, qkv, ctx, lse, wk, w_out, hot, cold, sums, up_sum, gr1, tokens,
            grad_up, grad_down, row_count, seq, shard,
        )
        mats = take_step(tot0, tot1, tot2, *state)
        vec_grads = totv[0, :shard]
        sizes = jnp.sum(totv[1:5, :LANES], axis=1)
    else:
        gqkv, bias_sums, part_in = attn_bwd(
            gattn, qkv, ctx, lse, w_project, w_out, hot, cold, row_count, seq
        )
        swap = [(0, 1), (1, 0)]
        input_grad = gr1 + part_in.astype(F32) + lax.ppermute(part_in, "tensor", swap).astype(F32)
        bias_pair = jnp.sum(bias_sums, axis=0)
        shared_sums = lax.dynamic_slice_in_dim(sums[:6], own_index * half, half, axis=1)
        vec_local = jnp.concatenate([bias_pair[:2].reshape(-1), up_sum[0], shared_sums.reshape(-1)])
        sizes = jnp.sum(sums[6:10], axis=1)
        grads = (tn(tokens, gqkv).astype(BF), tn(ctx, gattn).astype(BF), grad_up, grad_down)
        mats, vec_grads, sizes = far_step((*grads, vec_local, sizes), state)
    stream_rms = jnp.sqrt(sizes[:3] / (sizes[3] * width / LANES))
    second_new = DECAY * vec_second + (1.0 - DECAY) * vec_grads * vec_grads
    vec_new = vec_master - VEC_RATE * vec_grads / (jnp.sqrt(second_new) + VEC_EPS)
    return (block_out, input_grad, *mats, vec_grads, second_new, vec_new, stream_rms)


def solution(mesh):
    blocks = P(("dp", "tensor"), None, None)
    rows = P("dp", None)
    entries = P(("dp", "tensor"))
    return jax.shard_map(
        body,
        mesh=mesh,
        in_specs=(rows, rows, rows, *[blocks] * 5, entries, entries),
        out_specs=(rows, rows, *[blocks] * 4, entries, entries, entries, P()),
        check_vma=False,
    )
```
